32 devices in a mesh: dp: 4 (over x, core), sp: 4 (over z), blk: 2 (over y).
Axes of the slice: x: 2, y: 2, z: 4, core: 2. Of those that a mesh axis runs over, the one named last changes fastest.
Arguments:
- inputs: bfloat16 [8192, 1024], P(('dp', 'sp', 'blk')), may hold values from -6 to 6
- w_qkv: bfloat16 [1024, 3072], P(('dp', 'sp', 'blk')), may hold values from -0.1875 to 0.1875
- w_dense: bfloat16 [1024, 1024], P(('dp', 'sp', 'blk')), may hold values from -0.75 to 0.75
- w_in: bfloat16 [1024, 4096], P(('dp', 'sp', 'blk')), may hold values from -0.1875 to 0.1875
- w_out: bfloat16 [4096, 1024], P(('dp', 'sp', 'blk')), may hold values from -0.09375 to 0.09375
- norm_gains: bfloat16 [2, 1024], P(None, ('dp', 'sp', 'blk')), may hold values from 0.5 to 1.5
- biases: bfloat16 [6, 1024], P(None, ('dp', 'sp', 'blk')), may hold values from -3 to 3
- in_bias: bfloat16 [4096], P(('dp', 'sp', 'blk')), may hold values from -3 to 3
- alibi_slopes: float32 [16], replicated, may hold values from 0.00024414062 to 0.1
- upstream: bfloat16 [8192, 1024], P(('dp', 'sp', 'blk')), may hold values from -6 to 6
Outputs:
- output: bfloat16 [8192, 1024], P(('dp', 'sp', 'blk'))
- grad_inputs: float32 [8192, 1024], P(('dp', 'sp', 'blk'))
- grad_w_qkv: float32 [1024, 3072], P(('dp', 'sp', 'blk'))
- grad_w_dense: float32 [1024, 1024], P(('dp', 'sp', 'blk'))
- grad_w_in: float32 [1024, 4096], P(('dp', 'sp', 'blk'))
- grad_w_out: float32 [4096, 1024], P(('dp', 'sp', 'blk'))
- grad_norm_gains: float32 [2, 1024], P(None, ('dp', 'sp', 'blk'))
- grad_biases: float32 [6, 1024], P(None, ('dp', 'sp', 'blk'))
- grad_in_bias: float32 [4096], P(('dp', 'sp', 'blk'))
The draws below stay inside these ranges and needn't reach their ends.
All inputs are finite; a program needn't handle non-finite values.
Results may differ from the reference program's by a relative error of at most 0.0096.
Values may be sent and summed in bfloat16 or wider, within the bound.
No kernel may reach another device: no remote copies, remote signals or barrier semaphores. Data moves between devices by JAX's collectives and lax.ppermute only.
A program may use at most 192 MiB of HBM per device.

```python
import math
import jax
import jax.numpy as jnp
from jax import lax

D = 1024
H = 16
FF = 4096
SEQ_LEN = 2048
SEQS = 4
TOKENS = 8192


def spiked(values, rng, source, target, shards_of, factor):
    def block_of(axis_at):
        return (jnp.arange(values.shape[axis_at]) // (values.shape[axis_at] // shards_of)).reshape((-1,) + (1,) * (values.ndim - 1 - axis_at))

    one_side = jax.random.permutation(rng, shards_of)[block_of(target)]
    second = (block_of(target) + shards_of // 2) % shards_of
    return jnp.where((block_of(source) == one_side) | (block_of(source) == second), factor * values, values)


def steps_of(key, extent, shards, smallest, top_value):
    gain = 1.0
    for dim, parts in shards:
        heights = jax.random.uniform(jax.random.fold_in(jax.random.fold_in(key, 6), dim), (parts,), jnp.float32, smallest / len(shards), top_value / len(shards))
        gain = gain * jnp.repeat(jnp.exp(heights), extent[dim] // parts).reshape((-1,) + (1,) * (len(extent) - 1 - dim))
    return gain


def scatter_about(rng, dims, spread, limit, split=(), kind=jnp.bfloat16):
    loudness = steps_of(rng, dims, split, -0.22, 0.18) if split else 1.0
    entries = jax.random.normal(rng, dims, jnp.float32) * spread * loudness
    return jnp.minimum(jnp.maximum(entries, -limit), limit).astype(kind)


def heavy_noise(rng, shape, scale, bound, cuts, heavy, kind=jnp.bfloat16):
    values = scale * jax.random.normal(rng, shape, jnp.float32)
    if cuts:
        values = values * steps_of(rng, shape, cuts, -0.22, 0.18)
    return jnp.clip(spiked(values, jax.random.fold_in(rng, 3), *heavy), -bound, bound).astype(kind)


def setup_inputs(seed: int = 0) -> dict:
    key_of = jax.random.split(jax.random.key(seed), 11)
    return {
        "inputs": scatter_about(key_of[0], (TOKENS, D), 1.0, 6.0, ((0, 32),)),
        "w_qkv": scatter_about(key_of[1], (D, 3 * D), D ** -0.5, 0.1875, ((0, 32),)),
        "w_dense": scatter_about(key_of[2], (D, D), (D // 16) ** -0.5, 0.75, ((0, 32),)),
        "w_in": scatter_about(key_of[3], (D, FF), D ** -0.5, 0.1875, ((0, 32),)),
        "w_out": scatter_about(key_of[4], (FF, D), FF ** -0.5, 0.09375, ((0, 32),)),
        "norm_gains": jnp.clip(1.0 + 0.1 * jax.random.normal(key_of[5], (2, D), jnp.float32), 0.5, 1.5).astype(jnp.bfloat16),
        "biases": scatter_about(key_of[6], (6, D), 0.5, 3.0, ((1, 32),)),
        "in_bias": scatter_about(key_of[7], (FF,), 0.5, 3.0, ((0, 32),)),
        "alibi_slopes": jnp.clip(jnp.exp(jax.random.uniform(key_of[8], (H,), jnp.float32, math.log(0.00024414062), math.log(0.1))), 0.00024414062, 0.1),
        "upstream": heavy_noise(key_of[9], (TOKENS, D), 1.0, 6.0, ((0, 32),), (0, 1, 32, 2.75)),
    }


@jax.custom_vjp
def low(v):
    return lax.optimization_barrier(v.astype(jnp.bfloat16)).astype(jnp.float32)

@jax.custom_vjp
def low_back(v):
    return v

def low_keep(v):
    return (low(v), None)

def low_pass(kept, grad):
    return (grad,)

def back_keep(v):
    return (v, None)

def back_low(kept, grad):
    return (low(grad),)
low.defvjp(low_keep, low_pass)
low_back.defvjp(back_keep, back_low)

def norm_rows(features, gain_row, offset):
    row_mean = lax.optimization_barrier(jnp.mean(features, axis=-1, keepdims=True))
    centered = features - row_mean
    variance = lax.optimization_barrier(jnp.mean(centered * centered, axis=-1, keepdims=True))
    return centered * lax.rsqrt(variance + 1e-05) * gain_row + offset

def round_both(tensor):
    return low(low_back(tensor))

def attend_sequence(query_rows, key_rows, value_rows, slopes):
    length = query_rows.shape[0]
    block_rows = min(512, length)
    score_scale = 1.0 / math.sqrt(query_rows.shape[2])
    key_places = jnp.arange(length, dtype=jnp.int32)

    def one_block(first_row):
        chosen = lax.dynamic_slice_in_dim(query_rows, first_row, block_rows, 0)
        row_places = first_row + jnp.arange(block_rows, dtype=jnp.int32)
        scores = jnp.einsum('qhe,khe->hqk', chosen, key_rows, precision=lax.Precision.HIGHEST) * score_scale
        distance = (row_places[:, None] - key_places[None, :]).astype(jnp.float32)
        scores = scores - slopes[:, None, None] * distance[None]
        scores = jnp.where((distance >= 0)[None], scores, -1e+30)
        soft_weights = low(jax.nn.softmax(low_back(scores), axis=-1))
        return jnp.einsum('hqk,khe->qhe', soft_weights, value_rows, precision=lax.Precision.HIGHEST)
    firsts = jnp.arange(length // block_rows, dtype=jnp.int32) * block_rows
    pieces = lax.map(jax.checkpoint(one_block), firsts)
    return pieces.reshape(length, query_rows.shape[1], query_rows.shape[2])

def forward(inputs, w_qkv, w_dense, w_in, w_out, norm_gains, biases, in_bias, slopes):
    normed_one = low(norm_rows(inputs, norm_gains[0], biases[0]))
    projected = jnp.dot(normed_one, w_qkv, precision=lax.Precision.HIGHEST)
    query = round_both(projected[:, :D] + biases[1])
    key_all = round_both(projected[:, D:2 * D])
    value_all = round_both(projected[:, 2 * D:] + biases[2])
    layout = (SEQS, SEQ_LEN, H, D // H)

    def per_sequence(triple):
        return attend_sequence(triple[0], triple[1], triple[2], slopes)
    context = lax.map(per_sequence, (query.reshape(layout), key_all.reshape(layout), value_all.reshape(layout)))
    context = round_both(context.reshape(TOKENS, D))
    attended = low_back(jnp.dot(context, w_dense, precision=lax.Precision.HIGHEST) + biases[3])
    middle = inputs + attended
    normed_two = low(norm_rows(middle, norm_gains[1], biases[4]))
    hidden_pre = low_back(jnp.dot(normed_two, w_in, precision=lax.Precision.HIGHEST) + in_bias)
    hidden = low(jax.nn.gelu(hidden_pre))
    branch = low_back(jnp.dot(hidden, w_out, precision=lax.Precision.HIGHEST) + biases[5])
    return middle + branch

def reference(inputs, w_qkv, w_dense, w_in, w_out, norm_gains, biases, in_bias, alibi_slopes, upstream):
    primals = tuple((item.astype(jnp.float32) for item in (inputs, w_qkv, w_dense, w_in, w_out, norm_gains, biases, in_bias)))

    def apply_block(*params):
        return forward(*params, alibi_slopes)
    result, pullback = jax.vjp(apply_block, *primals)
    gradients = pullback(upstream.astype(jnp.float32))
    return (result.astype(jnp.bfloat16), gradients[0], gradients[1], gradients[2], gradients[3], gradients[4], gradients[5], gradients[6], gradients[7])
```

```python
import functools
import math

import jax
import jax.numpy as jnp
from jax import lax
from jax.experimental import pallas as pl
from jax.experimental.pallas import tpu as pltpu
from jax.sharding import PartitionSpec as P

H = 16
ALL = ("dp", "sp", "blk")
SEQ_AXES = ("sp", "blk")
F32 = jnp.float32
BF16 = jnp.bfloat16
LOG2E = 1.4426950408889634


def norm_rows(features, gain_row, offset):
    row_mean = jnp.mean(features, axis=-1, keepdims=True)
    centered = features - row_mean
    variance = jnp.mean(centered * centered, axis=-1, keepdims=True)
    return centered * lax.rsqrt(variance + 1e-05) * gain_row + offset


def dot_nn(a, b):
    return lax.dot_general(a, b, (((1,), (0,)), ((), ())), preferred_element_type=F32)


def dot_nt(a, b):
    return lax.dot_general(a, b, (((1,), (1,)), ((), ())), preferred_element_type=F32)


def dot_tn(a, b):
    return lax.dot_general(a, b, (((0,), (0,)), ((), ())), preferred_element_type=F32)


def exchange(value, bit):
    count = lax.axis_size("dp")
    return lax.ppermute(value, "dp", [(i, i ^ bit) for i in range(count)])


def gather_dp(value):
    pieces = {0: value}
    bit = lax.axis_size("dp") // 2
    while bit:
        for place in list(pieces):
            pieces[place | bit] = exchange(pieces[place], bit)
        bit //= 2
    return [pieces[place] for place in range(len(pieces))]


def swap_dp(pieces):
    return [pieces[0]] + [exchange(pieces[place], place) for place in range(1, len(pieces))]


def sum_dp(pieces):
    pieces = dict(enumerate(pieces))
    count, bit = len(pieces), 1
    while bit < count:
        for place in range(0, count, 2 * bit):
            arrived = exchange(pieces[place + bit].astype(BF16), bit)
            pieces[place] = pieces[place].astype(F32) + arrived.astype(F32)
        bit *= 2
    return pieces[0]


def one_head(rows, head, head_dim):
    lane = lax.broadcasted_iota(jnp.int32, rows.shape, 1)
    inside = (lane >= head * head_dim) & (lane < (head + 1) * head_dim)
    return jnp.where(inside, rows, jnp.zeros_like(rows))


def score_tile(keys, query_head, scale, slope, key_first, query_first, masked):
    scores = dot_nt(keys, query_head) * scale
    key_row = lax.broadcasted_iota(jnp.int32, (keys.shape[0], 1), 0)
    ahead = key_first - query_first
    scores = scores + (key_row.astype(F32) * slope + ahead.astype(F32) * slope)
    if masked:
        key_place = lax.broadcasted_iota(jnp.int32, scores.shape, 0) + ahead
        query_place = lax.broadcasted_iota(jnp.int32, scores.shape, 1)
        scores = jnp.where(key_place <= query_place, scores, -1e30)
    return scores


def forward_kernel(heads, head_dim, block, slopes_ref, qkv_ref, ctx_ref, ctx_t_ref, lse_ref, value_t_ref):
    width = heads * head_dim
    step = pl.program_id(0)
    scale = LOG2E / math.sqrt(head_dim)

    @pl.when(step == 0)
    def _():
        value_t_ref[...] = qkv_ref[:, 2 * width :].astype(F32).T.astype(BF16)

    first = pl.multiple_of(step * block, block)
    rows = qkv_ref[pl.ds(first, block), 0:width]
    queries = [one_head(rows, head, head_dim) for head in range(heads)]
    slopes = [slopes_ref[head] * LOG2E for head in range(heads)]

    def tile(index, running, masked):
        key_first = pl.multiple_of(index * block, block)
        keys = qkv_ref[pl.ds(key_first, block), width : 2 * width]
        values = value_t_ref[:, pl.ds(key_first, block)]
        after = []
        for head in range(heads):
            top, total, context = running[head]
            scores = score_tile(keys, queries[head], scale, slopes[head], key_first, first, masked)
            new_top = jnp.maximum(top, jnp.max(scores, axis=0, keepdims=True))
            exponent = jnp.exp2(scores - new_top)
            shrink = jnp.exp2(top - new_top)
            total = total * shrink + jnp.sum(exponent, axis=0, keepdims=True)
            part = dot_nn(values[head * head_dim : (head + 1) * head_dim], exponent.astype(BF16))
            after.append((new_top, total, context * shrink + part))
        return tuple(after)

    start = tuple(
        (jnp.full((1, block), -1e30, F32), jnp.zeros((1, block), F32), jnp.zeros((head_dim, block), F32))
        for _ in range(heads)
    )
    running = lax.fori_loop(0, step, lambda index, held: tile(index, held, False), start)
    running = tile(step, running, True)
    contexts = []
    for head in range(heads):
        top, total, context = running[head]
        context = context * (1.0 / total)
        ctx_t_ref[head * head_dim : (head + 1) * head_dim, pl.ds(first, block)] = context
        lse_ref[head : head + 1, pl.ds(first, block)] = top + jnp.log2(total)
        contexts.append(context)
    ctx_ref[pl.ds(first, block), :] = jnp.concatenate(contexts, axis=0).T.astype(BF16)


def backward_kernel(
    heads, head_dim, block, slopes_ref, qkv_ref, grad_ref, ctx_t_ref, lse_ref, out_ref, key_t_ref, grad_key_ref, grad_value_ref
):
    width = heads * head_dim
    step = pl.program_id(0)
    scale = LOG2E / math.sqrt(head_dim)
    unit = 1.0 / math.sqrt(head_dim)

    @pl.when(step == 0)
    def _():
        key_t_ref[...] = qkv_ref[:, width : 2 * width].astype(F32).T.astype(BF16)
        grad_key_ref[...] = jnp.zeros_like(grad_key_ref)
        grad_value_ref[...] = jnp.zeros_like(grad_value_ref)

    first = pl.multiple_of(step * block, block)
    rows = qkv_ref[pl.ds(first, block), 0:width]
    grad_rows = grad_ref[pl.ds(first, block), :]
    queries = [one_head(rows, head, head_dim) for head in range(heads)]
    grads = [one_head(grad_rows, head, head_dim) for head in range(heads)]
    product = grad_rows.astype(F32).T * ctx_t_ref[:, pl.ds(first, block)]
    deltas = [
        jnp.sum(product[head * head_dim : (head + 1) * head_dim], axis=0, keepdims=True)
        for head in range(heads)
    ]
    lses = [lse_ref[head : head + 1, pl.ds(first, block)] for head in range(heads)]
    slopes = [slopes_ref[head] * LOG2E for head in range(heads)]

    def tile(index, running, masked):
        key_first = pl.multiple_of(index * block, block)
        keys = qkv_ref[pl.ds(key_first, block), width : 2 * width]
        values = qkv_ref[pl.ds(key_first, block), 2 * width :]
        keys_t = key_t_ref[:, pl.ds(key_first, block)]
        grad_key = grad_key_ref[pl.ds(key_first, block), :]
        grad_value = grad_value_ref[pl.ds(key_first, block), :]
        after = []
        for head in range(heads):
            scores = score_tile(keys, queries[head], scale, slopes[head], key_first, first, masked)
            weights = jnp.exp2(scores - lses[head])
            grad_weights = dot_nt(values, grads[head])
            grad_scores = (weights * (grad_weights - deltas[head])).astype(BF16)
            grad_value = grad_value + dot_nn(weights.astype(BF16), grads[head])
            grad_key = grad_key + dot_nn(grad_scores, queries[head])
            head_rows = keys_t[head * head_dim : (head + 1) * head_dim]
            after.append(running[head] + dot_nn(head_rows, grad_scores))
        grad_key_ref[pl.ds(key_first, block), :] = grad_key
        grad_value_ref[pl.ds(key_first, block), :] = grad_value
        return tuple(after)

    start = tuple(jnp.zeros((head_dim, block), F32) for _ in range(heads))
    running = lax.fori_loop(0, step, lambda index, held: tile(index, held, False), start)
    running = tile(step, running, True)
    grad_query = jnp.concatenate(running, axis=0) * unit
    out_ref[pl.ds(first, block), 0:width] = grad_query.T.astype(BF16)

    @pl.when(step == pl.num_programs(0) - 1)
    def _():
        out_ref[:, width : 2 * width] = (grad_key_ref[...] * unit).astype(BF16)
        out_ref[:, 2 * width :] = grad_value_ref[...].astype(BF16)


def whole(count):
    return [pl.BlockSpec(memory_space=pltpu.VMEM)] * count


def attend_forward(slopes, qkv, heads, block):
    length, width = qkv.shape[0], qkv.shape[1] // 3
    head_dim = width // heads
    pairs = heads * length * length
    return pl.pallas_call(
        functools.partial(forward_kernel, heads, head_dim, block),
        grid=(length // block,),
        out_shape=(
            jax.ShapeDtypeStruct((length, width), BF16),
            jax.ShapeDtypeStruct((width, length), F32),
            jax.ShapeDtypeStruct((heads, length), F32),
        ),
        in_specs=[pl.BlockSpec(memory_space=pltpu.SMEM)] + whole(1),
        out_specs=tuple(whole(3)),
        scratch_shapes=[pltpu.VMEM((width, length), BF16)],
        compiler_params=pltpu.CompilerParams(vmem_limit_bytes=40 << 20),
        cost_estimate=pl.CostEstimate(
            flops=4 * pairs * head_dim, bytes_accessed=6 * length * width, transcendentals=pairs
        ),
        name="attend_forward",
    )(slopes, qkv)


def attend_backward(slopes, qkv, grad, ctx_t, lse, heads, block):
    length, width = qkv.shape[0], qkv.shape[1] // 3
    head_dim = width // heads
    pairs = heads * length * length
    return pl.pallas_call(
        functools.partial(backward_kernel, heads, head_dim, block),
        grid=(length // block,),
        out_shape=jax.ShapeDtypeStruct((length, 3 * width), BF16),
        in_specs=[pl.BlockSpec(memory_space=pltpu.SMEM)] + whole(4),
        out_specs=whole(1)[0],
        scratch_shapes=[
            pltpu.VMEM((width, length), BF16),
            pltpu.VMEM((length, width), F32),
            pltpu.VMEM((length, width), F32),
        ],
        compiler_params=pltpu.CompilerParams(vmem_limit_bytes=40 << 20),
        cost_estimate=pl.CostEstimate(
            flops=10 * pairs * head_dim, bytes_accessed=12 * length * width, transcendentals=pairs
        ),
        name="attend_backward",
    )(slopes, qkv, grad, ctx_t, lse)


def split_scores(query_rows, row_places, key_rows, key_places, slopes, score_scale):
    scores = jnp.einsum("qhe,khe->hqk", query_rows, key_rows, preferred_element_type=F32) * score_scale
    distance = (row_places[:, None] - key_places[None, :]).astype(F32)
    scores = scores - slopes[:, None, None] * distance[None]
    return jnp.where((distance >= 0)[None], scores, -1e30)


def split_setup(qkv, heads, rows_each):
    local, width = qkv.shape[0], qkv.shape[1] // 3
    shape = (heads, width // heads)
    parts, mine = lax.axis_size("blk"), lax.axis_index("blk")
    held = lax.all_gather(qkv[:, width:], "blk", axis=0, tiled=False)
    held = held.reshape(parts, local // rows_each, rows_each, 2 * width).transpose(1, 0, 2, 3)
    held = held.reshape(parts * local, 2 * width)
    index = jnp.arange(local, dtype=jnp.int32)
    places = (index // rows_each * parts + mine) * rows_each + index % rows_each
    block = min(512, local)
    return (
        qkv[:, :width].reshape((local // block, block) + shape),
        held[:, :width].reshape((parts * local,) + shape),
        held[:, width:].reshape((parts * local,) + shape),
        places.reshape(local // block, block),
        jnp.arange(parts * local, dtype=jnp.int32),
        1.0 / math.sqrt(width // heads),
    )


def split_forward(slopes, qkv, heads, rows_each):
    queries, keys, values, places, key_places, scale = split_setup(qkv, heads, rows_each)

    def one_block(item):
        chosen, block_places = item
        scores = split_scores(chosen, block_places, keys, key_places, slopes, scale)
        top = jnp.max(scores, axis=-1, keepdims=True)
        exponent = jnp.exp(scores - top)
        total = jnp.sum(exponent, axis=-1, keepdims=True)
        weights = (exponent / total).astype(BF16)
        context = jnp.einsum("hqk,khe->qhe", weights, values, preferred_element_type=F32)
        return context.astype(BF16), top, total

    contexts, tops, totals = lax.map(one_block, (queries, places))
    return contexts.reshape(qkv.shape[0], -1), tops, totals


def split_backward(slopes, qkv, grad, tops, totals, heads, rows_each):
    queries, keys, values, places, key_places, scale = split_setup(qkv, heads, rows_each)
    grads = grad.reshape(queries.shape)

    def one_block(running, item):
        grad_keys, grad_values = running
        chosen, block_places, grad_rows, top, total = item
        scores = split_scores(chosen, block_places, keys, key_places, slopes, scale)
        weights = jnp.exp(scores - top) / total
        grad_values = grad_values + jnp.einsum(
            "hqk,qhe->khe", weights.astype(BF16), grad_rows, preferred_element_type=F32
        )
        grad_probs = jnp.einsum("qhe,khe->hqk", grad_rows, values, preferred_element_type=F32)
        grad_scores = (
            weights * (grad_probs - jnp.sum(weights * grad_probs, axis=-1, keepdims=True))
        ).astype(BF16)
        grad_query = jnp.einsum("hqk,khe->qhe", grad_scores, keys, preferred_element_type=F32) * scale
        grad_keys = (
            grad_keys
            + jnp.einsum("hqk,qhe->khe", grad_scores, chosen, preferred_element_type=F32) * scale
        )
        return (grad_keys, grad_values), grad_query.astype(BF16)

    empty = jnp.zeros(keys.shape, F32)
    (grad_keys, grad_values), grad_queries = lax.scan(
        one_block, (empty, empty), (queries, places, grads, tops, totals)
    )
    local, width = grad.shape
    both = jnp.concatenate([grad_keys.reshape(-1, width), grad_values.reshape(-1, width)], axis=1)
    parts = lax.axis_size("blk")
    both = both.reshape(local // rows_each, parts, rows_each, 2 * width).transpose(1, 0, 2, 3)
    own = lax.psum_scatter(both, "blk", scatter_dimension=0, tiled=False)
    own = own.reshape(local, 2 * width).astype(BF16)
    return jnp.concatenate([grad_queries.reshape(local, width), own], axis=1)


def on_device(
    inputs, w_qkv, w_dense, w_in, w_out, norm_gains, biases, in_bias, alibi_slopes, upstream
):
    dp_count, sp_count, blk_count = (lax.axis_size(axis) for axis in ALL)
    dp_place = lax.axis_index("dp")
    ring = sp_count * blk_count
    devices = dp_count * ring
    rows, width = inputs.shape
    slice_rows = w_qkv.shape[0]
    inner = in_bias.shape[0] * devices // dp_count
    head_dim = width // H
    dp_heads = H // dp_count
    dp_width = dp_heads * head_dim

    whole_pairs = ring % dp_count == 0 and dp_heads % max(1, ring // dp_count) == 0
    pair_axes = SEQ_AXES if whole_pairs else ("sp",)
    owners = ring if whole_pairs else sp_count
    groups = owners // dp_count
    pair_heads = dp_heads // groups
    pair_width = pair_heads * head_dim

    def spread(pieces):
        columns = pieces.shape[-1]
        sent = pieces.transpose(0, 2, 1, 3).reshape(owners * rows, columns)
        return lax.all_to_all(sent, pair_axes, split_axis=0, concat_axis=0, tiled=True)

    def collect(held):
        columns = held.shape[-1]
        got = lax.all_to_all(held, pair_axes, split_axis=0, concat_axis=0, tiled=True)
        return got.reshape(dp_count, groups, rows, columns).transpose(0, 2, 1, 3)

    tokens = jnp.concatenate(gather_dp(inputs), axis=0)
    grad_tokens = jnp.concatenate(gather_dp(upstream), axis=0)
    small = jnp.concatenate([norm_gains.reshape(-1), biases.reshape(-1), in_bias])
    small = lax.all_to_all(
        jnp.broadcast_to(small[None], (devices, small.shape[0])), ALL, split_axis=0, concat_axis=0, tiled=True
    )
    gain_size, bias_size = norm_gains.size, biases.size
    gains_row = small[:, :gain_size].reshape(devices, 2, -1).transpose(1, 0, 2).reshape(2, width).astype(F32)
    offsets = small[:, gain_size : gain_size + bias_size].reshape(devices, 6, -1)
    offsets = offsets.transpose(1, 0, 2).reshape(6, width).astype(F32)
    in_offset = lax.dynamic_slice_in_dim(
        small[:, gain_size + bias_size :].reshape(-1), dp_place * inner, inner
    ).astype(F32)

    def columns_weight(pieces):
        columns = pieces.shape[-1]
        swapped = lax.all_to_all(pieces, "dp", split_axis=0, concat_axis=0, tiled=True)
        gathered = lax.all_gather(swapped, SEQ_AXES, axis=0, tiled=False)
        return gathered.transpose(1, 0, 2, 3).reshape(width, columns)

    def columns_gradient(grad):
        columns = grad.shape[-1]
        sent = grad.astype(BF16).reshape(dp_count, ring, slice_rows, columns).transpose(1, 0, 2, 3)
        summed = lax.psum_scatter(sent, SEQ_AXES, scatter_dimension=0, tiled=False)
        return lax.all_to_all(summed, "dp", split_axis=0, concat_axis=0, tiled=True)

    qkv_split = w_qkv.reshape(slice_rows, 3, dp_count, groups, pair_width).transpose(2, 0, 3, 1, 4)
    qkv_weight = columns_weight(qkv_split.reshape(dp_count, slice_rows, 3 * dp_width))
    dense_part = lax.all_gather(w_dense, SEQ_AXES, axis=0, tiled=True)
    in_weight = columns_weight(w_in.reshape(slice_rows, dp_count, inner).transpose(1, 0, 2))
    out_weight = lax.all_gather(w_out, SEQ_AXES, axis=0, tiled=True)
    dense_weight = jnp.concatenate(gather_dp(dense_part), axis=0)

    rows_in = inputs.astype(F32)
    normed_one = norm_rows(tokens.astype(F32), gains_row[0], offsets[0]).astype(BF16)
    own_offset = lax.dynamic_slice_in_dim(offsets, dp_place * dp_width, dp_width, 1)
    own_offset = own_offset.reshape(6, groups, pair_width)
    qkv_offset = jnp.stack([own_offset[1], jnp.zeros_like(own_offset[1]), own_offset[2]], axis=1).reshape(-1)
    projected = (dot_nn(normed_one, qkv_weight) + qkv_offset).astype(BF16)
    qkv = spread(projected.reshape(dp_count, rows, groups, 3 * pair_width))
    group = lax.axis_index(pair_axes) % groups
    slopes = lax.dynamic_slice_in_dim(alibi_slopes, dp_place * dp_heads + group * pair_heads, pair_heads)
    if whole_pairs:
        block = min(512, ring * rows)
        context, *kept = attend_forward(slopes, qkv, pair_heads, block)
    else:
        context, *kept = split_forward(slopes, qkv, pair_heads, rows)
    context_tok = collect(context).reshape(dp_count, rows, dp_width)
    context_tok = jnp.concatenate(swap_dp([context_tok[k] for k in range(dp_count)]), axis=1)
    middle = rows_in + (dot_nn(context_tok, dense_weight) + offsets[3])
    normed_two = norm_rows(middle, gains_row[1], offsets[4]).astype(BF16)
    normed_two_all = jnp.concatenate(gather_dp(normed_two), axis=0)
    hidden_pre = dot_nn(normed_two_all, in_weight) + in_offset
    hidden, gelu_pull = jax.vjp(jax.nn.gelu, hidden_pre)
    hidden = hidden.astype(BF16)

    grad_top = upstream.astype(F32)
    grad_pre = gelu_pull(dot_nt(grad_tokens, out_weight))[0].astype(BF16)
    grad_normed_two = sum_dp(list(dot_nt(grad_pre, in_weight).reshape(dp_count, rows, width)))
    _, second_pull = jax.vjp(norm_rows, middle, gains_row[1], offsets[4])
    grad_mid_part, grad_gain_two, grad_shift_two = second_pull(grad_normed_two)
    grad_middle = grad_top + grad_mid_part
    grad_att = grad_middle.astype(BF16)
    grad_context = dot_nt(grad_att, dense_weight).astype(BF16)
    grad_context = swap_dp([grad_context[:, k * dp_width : (k + 1) * dp_width] for k in range(dp_count)])
    grad_held = spread(jnp.stack(grad_context).reshape(dp_count, rows, groups, pair_width))

    branch = sum_dp(list(dot_nn(hidden, out_weight).reshape(dp_count, rows, width)))
    output = (middle + (branch + offsets[5])).astype(BF16)
    grad_w_out = lax.psum_scatter(
        dot_tn(hidden, grad_tokens).astype(BF16), SEQ_AXES, scatter_dimension=0, tiled=True
    ).astype(F32)
    grad_w_in = columns_gradient(dot_tn(normed_two_all, grad_pre))
    grad_w_in = grad_w_in.transpose(1, 0, 2).reshape(slice_rows, -1).astype(F32)
    grad_dense = sum_dp(list(dot_tn(context_tok, grad_att).reshape(dp_count, dp_width, width)))
    grad_w_dense = lax.psum_scatter(
        grad_dense.astype(BF16), SEQ_AXES, scatter_dimension=0, tiled=True
    ).astype(F32)

    if whole_pairs:
        grad_qkv = attend_backward(slopes, qkv, grad_held, *kept, pair_heads, block)
    else:
        grad_qkv = split_backward(slopes, qkv, grad_held, *kept, pair_heads, rows)
    grad_projected = collect(grad_qkv).reshape(dp_count * rows, 3 * dp_width)
    grad_w_qkv = columns_gradient(dot_tn(normed_one, grad_projected))
    grad_w_qkv = grad_w_qkv.reshape(dp_count, slice_rows, groups, 3, pair_width).transpose(1, 3, 0, 2, 4)
    grad_w_qkv = grad_w_qkv.reshape(slice_rows, 3 * width).astype(F32)
    grad_normed_one = sum_dp(list(dot_nt(grad_projected, qkv_weight).reshape(dp_count, rows, width)))
    _, first_pull = jax.vjp(norm_rows, rows_in, gains_row[0], offsets[0])
    grad_rows_part, grad_gain_one, grad_shift_one = first_pull(grad_normed_one)
    grad_inputs = grad_middle + grad_rows_part

    own_sums = jnp.sum(grad_projected.astype(F32), axis=0).reshape(groups, 3, pair_width)

    def placed(part, size):
        return lax.dynamic_update_slice_in_dim(jnp.zeros(size, F32), part, dp_place * part.shape[0], 0)

    grad_vectors = jnp.stack(
        [
            grad_gain_one,
            grad_gain_two,
            grad_shift_one,
            placed(own_sums[:, 0].reshape(-1), width),
            placed(own_sums[:, 2].reshape(-1), width),
            jnp.sum(grad_att.astype(F32), axis=0),
            grad_shift_two,
            jnp.sum(grad_top, axis=0),
        ]
    )
    grad_in_part = placed(jnp.sum(grad_pre.astype(F32), axis=0), inner * dp_count)
    parts = jnp.concatenate(
        [
            grad_vectors.reshape(8, devices, -1).transpose(1, 0, 2).reshape(devices, -1),
            grad_in_part.reshape(devices, -1),
        ],
        axis=1,
    )
    parts = lax.all_to_all(parts, ALL, split_axis=0, concat_axis=0, tiled=True)
    summed = jnp.sum(parts, axis=0)
    vectors = summed[: gain_size + bias_size].reshape(8, -1)
    return (
        output,
        grad_inputs,
        grad_w_qkv,
        grad_w_dense,
        grad_w_in,
        grad_w_out,
        vectors[:2],
        vectors[2:],
        summed[gain_size + bias_size :],
    )


def solution(mesh):
    rows, columns, vector = P(ALL, None), P(None, ALL), P(ALL)
    in_specs = (rows, rows, rows, rows, rows, columns, columns, vector, P(), rows)
    out_specs = (rows, rows, rows, rows, rows, rows, columns, columns, vector)
    return jax.shard_map(
        on_device, mesh=mesh, in_specs=in_specs, out_specs=out_specs, check_vma=False
    )
```

```python
import functools
import math

import jax
import jax.numpy as jnp
from jax import lax
from jax.experimental import pallas as pl
from jax.experimental.pallas import tpu as pltpu
from jax.sharding import PartitionSpec as P

H = 16
ALL = ("dp", "sp", "blk")
SEQ_AXES = ("sp", "blk")
F32 = jnp.float32
BF16 = jnp.bfloat16
LOG2E = 1.4426950408889634


def norm_rows(features, gain_row, offset):
    row_mean = jnp.mean(features, axis=-1, keepdims=True)
    centered = features - row_mean
    variance = jnp.mean(centered * centered, axis=-1, keepdims=True)
    return centered * lax.rsqrt(variance + 1e-05) * gain_row + offset


def dot_nn(a, b):
    return lax.dot_general(a, b, (((1,), (0,)), ((), ())), preferred_element_type=F32)


def dot_nt(a, b):
    return lax.dot_general(a, b, (((1,), (1,)), ((), ())), preferred_element_type=F32)


def dot_tn(a, b):
    return lax.dot_general(a, b, (((0,), (0,)), ((), ())), preferred_element_type=F32)


def exchange(value, bit, axis="dp"):
    count = lax.axis_size(axis)
    return lax.ppermute(value, axis, [(i, i ^ bit) for i in range(count)])


def gather_dp(value):
    pieces = {0: value}
    bit = lax.axis_size("dp") // 2
    while bit:
        for place in list(pieces):
            pieces[place | bit] = exchange(pieces[place], bit)
        bit //= 2
    return [pieces[place] for place in range(len(pieces))]


def swap_dp(pieces):
    return [pieces[0]] + [exchange(pieces[place], place) for place in range(1, len(pieces))]


def sum_dp(pieces):
    pieces = dict(enumerate(pieces))
    count, bit = len(pieces), 1
    while bit < count:
        for place in range(0, count, 2 * bit):
            arrived = exchange(pieces[place + bit].astype(BF16), bit)
            pieces[place] = pieces[place].astype(F32) + arrived.astype(F32)
        bit *= 2
    return pieces[0]


def to_places_dp(pieces):
    mine = lax.axis_index("dp")
    placed = pieces
    for place in range(1, pieces.shape[0]):
        other = mine ^ place
        arrived = exchange(lax.dynamic_index_in_dim(pieces, other, 0), place)
        placed = lax.dynamic_update_slice_in_dim(placed, arrived, other, 0)
    return placed


def sum_sequence(parts):
    held = parts.reshape((lax.axis_size("sp"), lax.axis_size("blk")) + parts.shape[1:])
    for axis, level in (("blk", 1), ("sp", 0)):
        place, bit = lax.axis_index(axis), 1
        while bit < lax.axis_size(axis):
            shape = held.shape
            halves = held.reshape(shape[:level] + (shape[level] // 2, 2) + shape[level + 1 :])
            side = place // bit % 2
            sent = lax.dynamic_index_in_dim(halves, 1 - side, level + 1, keepdims=False)
            kept = lax.dynamic_index_in_dim(halves, side, level + 1, keepdims=False)
            arrived = exchange(sent.astype(BF16), bit, axis)
            held = (kept.astype(F32) + arrived.astype(F32)).astype(BF16)
            bit *= 2
    return held.reshape(parts.shape[1:])


def one_head(rows, head, head_dim):
    lane = lax.broadcasted_iota(jnp.int32, rows.shape, 1)
    inside = (lane >= head * head_dim) & (lane < (head + 1) * head_dim)
    return jnp.where(inside, rows, jnp.zeros_like(rows))


def score_tile(keys, query_head, scale, slope, key_first, query_first, masked):
    scores = dot_nt(keys, query_head) * scale
    key_row = lax.broadcasted_iota(jnp.int32, (keys.shape[0], 1), 0)
    ahead = key_first - query_first
    scores = scores + (key_row.astype(F32) * slope + ahead.astype(F32) * slope)
    if masked:
        key_place = lax.broadcasted_iota(jnp.int32, scores.shape, 0) + ahead
        query_place = lax.broadcasted_iota(jnp.int32, scores.shape, 1)
        scores = jnp.where(key_place <= query_place, scores, -1e30)
    return scores


def forward_kernel(heads, head_dim, block, slopes_ref, qkv_ref, ctx_ref, ctx_t_ref, lse_ref, value_t_ref):
    width = heads * head_dim
    step = pl.program_id(0)
    scale = LOG2E / math.sqrt(head_dim)

    @pl.when(step == 0)
    def _():
        value_t_ref[...] = qkv_ref[:, 2 * width :].astype(F32).T.astype(BF16)

    first = pl.multiple_of(step * block, block)
    rows = qkv_ref[pl.ds(first, block), 0:width]
    queries = [one_head(rows, head, head_dim) for head in range(heads)]
    slopes = [slopes_ref[head] * LOG2E for head in range(heads)]

    def tile(index, running, masked):
        key_first = pl.multiple_of(index * block, block)
        keys = qkv_ref[pl.ds(key_first, block), width : 2 * width]
        values = value_t_ref[:, pl.ds(key_first, block)]
        after = []
        for head in range(heads):
            top, total, context = running[head]
            scores = score_tile(keys, queries[head], scale, slopes[head], key_first, first, masked)
            new_top = jnp.maximum(top, jnp.max(scores, axis=0, keepdims=True))
            exponent = jnp.exp2(scores - new_top)
            shrink = jnp.exp2(top - new_top)
            total = total * shrink + jnp.sum(exponent, axis=0, keepdims=True)
            part = dot_nn(values[head * head_dim : (head + 1) * head_dim], exponent.astype(BF16))
            after.append((new_top, total, context * shrink + part))
        return tuple(after)

    start = tuple(
        (jnp.full((1, block), -1e30, F32), jnp.zeros((1, block), F32), jnp.zeros((head_dim, block), F32))
        for _ in range(heads)
    )
    running = lax.fori_loop(0, step, lambda index, held: tile(index, held, False), start)
    running = tile(step, running, True)
    contexts = []
    for head in range(heads):
        top, total, context = running[head]
        context = context * (1.0 / total)
        ctx_t_ref[head * head_dim : (head + 1) * head_dim, pl.ds(first, block)] = context
        lse_ref[head : head + 1, pl.ds(first, block)] = top + jnp.log2(total)
        contexts.append(context)
    ctx_ref[pl.ds(first, block), :] = jnp.concatenate(contexts, axis=0).T.astype(BF16)


def backward_kernel(
    heads, head_dim, block, slopes_ref, qkv_ref, grad_ref, ctx_t_ref, lse_ref, out_ref, key_t_ref, grad_key_ref, grad_value_ref
):
    width = heads * head_dim
    step = pl.program_id(0)
    scale = LOG2E / math.sqrt(head_dim)
    unit = 1.0 / math.sqrt(head_dim)

    @pl.when(step == 0)
    def _():
        key_t_ref[...] = qkv_ref[:, width : 2 * width].astype(F32).T.astype(BF16)
        grad_key_ref[...] = jnp.zeros_like(grad_key_ref)
        grad_value_ref[...] = jnp.zeros_like(grad_value_ref)

    first = pl.multiple_of(step * block, block)
    rows = qkv_ref[pl.ds(first, block), 0:width]
    grad_rows = grad_ref[pl.ds(first, block), :]
    queries = [one_head(rows, head, head_dim) for head in range(heads)]
    grads = [one_head(grad_rows, head, head_dim) for head in range(heads)]
    product = grad_rows.astype(F32).T * ctx_t_ref[:, pl.ds(first, block)]
    deltas = [
        jnp.sum(product[head * head_dim : (head + 1) * head_dim], axis=0, keepdims=True)
        for head in range(heads)
    ]
    lses = [lse_ref[head : head + 1, pl.ds(first, block)] for head in range(heads)]
    slopes = [slopes_ref[head] * LOG2E for head in range(heads)]

    def tile(index, running, masked):
        key_first = pl.multiple_of(index * block, block)
        keys = qkv_ref[pl.ds(key_first, block), width : 2 * width]
        values = qkv_ref[pl.ds(key_first, block), 2 * width :]
        keys_t = key_t_ref[:, pl.ds(key_first, block)]
        grad_key = grad_key_ref[pl.ds(key_first, block), :]
        grad_value = grad_value_ref[pl.ds(key_first, block), :]
        after = []
        for head in range(heads):
            scores = score_tile(keys, queries[head], scale, slopes[head], key_first, first, masked)
            weights = jnp.exp2(scores - lses[head])
            grad_weights = dot_nt(values, grads[head])
            grad_scores = (weights * (grad_weights - deltas[head])).astype(BF16)
            grad_value = grad_value + dot_nn(weights.astype(BF16), grads[head])
            grad_key = grad_key + dot_nn(grad_scores, queries[head])
            head_rows = keys_t[head * head_dim : (head + 1) * head_dim]
            after.append(running[head] + dot_nn(head_rows, grad_scores))
        grad_key_ref[pl.ds(key_first, block), :] = grad_key
        grad_value_ref[pl.ds(key_first, block), :] = grad_value
        return tuple(after)

    start = tuple(jnp.zeros((head_dim, block), F32) for _ in range(heads))
    running = lax.fori_loop(0, step, lambda index, held: tile(index, held, False), start)
    running = tile(step, running, True)
    grad_query = jnp.concatenate(running, axis=0) * unit
    out_ref[pl.ds(first, block), 0:width] = grad_query.T.astype(BF16)

    @pl.when(step == pl.num_programs(0) - 1)
    def _():
        out_ref[:, width : 2 * width] = (grad_key_ref[...] * unit).astype(BF16)
        out_ref[:, 2 * width :] = grad_value_ref[...].astype(BF16)


def whole(count):
    return [pl.BlockSpec(memory_space=pltpu.VMEM)] * count


def attend_forward(slopes, qkv, heads, block):
    length, width = qkv.shape[0], qkv.shape[1] // 3
    head_dim = width // heads
    pairs = heads * length * length
    return pl.pallas_call(
        functools.partial(forward_kernel, heads, head_dim, block),
        grid=(length // block,),
        out_shape=(
            jax.ShapeDtypeStruct((length, width), BF16),
            jax.ShapeDtypeStruct((width, length), F32),
            jax.ShapeDtypeStruct((heads, length), F32),
        ),
        in_specs=[pl.BlockSpec(memory_space=pltpu.SMEM)] + whole(1),
        out_specs=tuple(whole(3)),
        scratch_shapes=[pltpu.VMEM((width, length), BF16)],
        compiler_params=pltpu.CompilerParams(vmem_limit_bytes=40 << 20),
        cost_estimate=pl.CostEstimate(
            flops=4 * pairs * head_dim, bytes_accessed=6 * length * width, transcendentals=pairs
        ),
        name="attend_forward",
    )(slopes, qkv)


def attend_backward(slopes, qkv, grad, ctx_t, lse, heads, block):
    length, width = qkv.shape[0], qkv.shape[1] // 3
    head_dim = width // heads
    pairs = heads * length * length
    return pl.pallas_call(
        functools.partial(backward_kernel, heads, head_dim, block),
        grid=(length // block,),
        out_shape=jax.ShapeDtypeStruct((length, 3 * width), BF16),
        in_specs=[pl.BlockSpec(memory_space=pltpu.SMEM)] + whole(4),
        out_specs=whole(1)[0],
        scratch_shapes=[
            pltpu.VMEM((width, length), BF16),
            pltpu.VMEM((length, width), F32),
            pltpu.VMEM((length, width), F32),
        ],
        compiler_params=pltpu.CompilerParams(vmem_limit_bytes=40 << 20),
        cost_estimate=pl.CostEstimate(
            flops=10 * pairs * head_dim, bytes_accessed=12 * length * width, transcendentals=pairs
        ),
        name="attend_backward",
    )(slopes, qkv, grad, ctx_t, lse)


def split_scores(query_rows, row_places, key_rows, key_places, slopes, score_scale):
    scores = jnp.einsum("qhe,khe->hqk", query_rows, key_rows, preferred_element_type=F32) * score_scale
    distance = (row_places[:, None] - key_places[None, :]).astype(F32)
    scores = scores - slopes[:, None, None] * distance[None]
    return jnp.where((distance >= 0)[None], scores, -1e30)


def split_setup(qkv, heads, rows_each):
    local, width = qkv.shape[0], qkv.shape[1] // 3
    shape = (heads, width // heads)
    parts, mine = lax.axis_size("blk"), lax.axis_index("blk")
    held = lax.all_gather(qkv[:, width:], "blk", axis=0, tiled=False)
    held = held.reshape(parts, local // rows_each, rows_each, 2 * width).transpose(1, 0, 2, 3)
    held = held.reshape(parts * local, 2 * width)
    index = jnp.arange(local, dtype=jnp.int32)
    places = (index // rows_each * parts + mine) * rows_each + index % rows_each
    block = min(512, local)
    return (
        qkv[:, :width].reshape((local // block, block) + shape),
        held[:, :width].reshape((parts * local,) + shape),
        held[:, width:].reshape((parts * local,) + shape),
        places.reshape(local // block, block),
        jnp.arange(parts * local, dtype=jnp.int32),
        1.0 / math.sqrt(width // heads),
    )


def split_forward(slopes, qkv, heads, rows_each):
    queries, keys, values, places, key_places, scale = split_setup(qkv, heads, rows_each)

    def one_block(item):
        chosen, block_places = item
        scores = split_scores(chosen, block_places, keys, key_places, slopes, scale)
        top = jnp.max(scores, axis=-1, keepdims=True)
        exponent = jnp.exp(scores - top)
        total = jnp.sum(exponent, axis=-1, keepdims=True)
        weights = (exponent / total).astype(BF16)
        context = jnp.einsum("hqk,khe->qhe", weights, values, preferred_element_type=F32)
        return context.astype(BF16), top, total

    contexts, tops, totals = lax.map(one_block, (queries, places))
    return contexts.reshape(qkv.shape[0], -1), tops, totals


def split_backward(slopes, qkv, grad, tops, totals, heads, rows_each):
    queries, keys, values, places, key_places, scale = split_setup(qkv, heads, rows_each)
    grads = grad.reshape(queries.shape)

    def one_block(running, item):
        grad_keys, grad_values = running
        chosen, block_places, grad_rows, top, total = item
        scores = split_scores(chosen, block_places, keys, key_places, slopes, scale)
        weights = jnp.exp(scores - top) / total
        grad_values = grad_values + jnp.einsum(
            "hqk,qhe->khe", weights.astype(BF16), grad_rows, preferred_element_type=F32
        )
        grad_probs = jnp.einsum("qhe,khe->hqk", grad_rows, values, preferred_element_type=F32)
        grad_scores = (
            weights * (grad_probs - jnp.sum(weights * grad_probs, axis=-1, keepdims=True))
        ).astype(BF16)
        grad_query = jnp.einsum("hqk,khe->qhe", grad_scores, keys, preferred_element_type=F32) * scale
        grad_keys = (
            grad_keys
            + jnp.einsum("hqk,qhe->khe", grad_scores, chosen, preferred_element_type=F32) * scale
        )
        return (grad_keys, grad_values), grad_query.astype(BF16)

    empty = jnp.zeros(keys.shape, F32)
    (grad_keys, grad_values), grad_queries = lax.scan(
        one_block, (empty, empty), (queries, places, grads, tops, totals)
    )
    local, width = grad.shape
    both = jnp.concatenate([grad_keys.reshape(-1, width), grad_values.reshape(-1, width)], axis=1)
    parts = lax.axis_size("blk")
    both = both.reshape(local // rows_each, parts, rows_each, 2 * width).transpose(1, 0, 2, 3)
    own = lax.psum_scatter(both, "blk", scatter_dimension=0, tiled=False)
    own = own.reshape(local, 2 * width).astype(BF16)
    return jnp.concatenate([grad_queries.reshape(local, width), own], axis=1)


def on_device(
    inputs, w_qkv, w_dense, w_in, w_out, norm_gains, biases, in_bias, alibi_slopes, upstream
):
    dp_count, sp_count, blk_count = (lax.axis_size(axis) for axis in ALL)
    dp_place = lax.axis_index("dp")
    ring = sp_count * blk_count
    devices = dp_count * ring
    rows, width = inputs.shape
    slice_rows = w_qkv.shape[0]
    inner = in_bias.shape[0] * devices // dp_count
    head_dim = width // H
    dp_heads = H // dp_count
    dp_width = dp_heads * head_dim

    whole_pairs = ring % dp_count == 0 and dp_heads % max(1, ring // dp_count) == 0
    pair_axes = SEQ_AXES if whole_pairs else ("sp",)
    owners = ring if whole_pairs else sp_count
    groups = owners // dp_count
    pair_heads = dp_heads // groups
    pair_width = pair_heads * head_dim

    def spread(pieces):
        columns = pieces.shape[-1]
        sent = pieces.transpose(0, 2, 1, 3).reshape(owners * rows, columns)
        return lax.all_to_all(sent, pair_axes, split_axis=0, concat_axis=0, tiled=True)

    def collect(held):
        columns = held.shape[-1]
        got = lax.all_to_all(held, pair_axes, split_axis=0, concat_axis=0, tiled=True)
        return got.reshape(dp_count, groups, rows, columns).transpose(0, 2, 1, 3)

    tokens = jnp.concatenate(gather_dp(inputs), axis=0)
    grad_tokens = jnp.concatenate(gather_dp(upstream), axis=0)
    small = jnp.concatenate([norm_gains.reshape(-1), biases.reshape(-1), in_bias])
    small = lax.all_to_all(
        jnp.broadcast_to(small[None], (devices, small.shape[0])), ALL, split_axis=0, concat_axis=0, tiled=True
    )
    gain_size, bias_size = norm_gains.size, biases.size
    gains_row = small[:, :gain_size].reshape(devices, 2, -1).transpose(1, 0, 2).reshape(2, width).astype(F32)
    offsets = small[:, gain_size : gain_size + bias_size].reshape(devices, 6, -1)
    offsets = offsets.transpose(1, 0, 2).reshape(6, width).astype(F32)
    in_offset = lax.dynamic_slice_in_dim(
        small[:, gain_size + bias_size :].reshape(-1), dp_place * inner, inner
    ).astype(F32)

    def my_columns(pieces):
        return lax.all_to_all(pieces, "dp", split_axis=0, concat_axis=0, tiled=True)

    def all_rows(gathered):
        columns = gathered.shape[-1]
        gathered = gathered.reshape(ring, dp_count, slice_rows, columns)
        return gathered.transpose(1, 0, 2, 3).reshape(width, columns)

    def columns_gradient(grad):
        columns = grad.shape[-1]
        parts = grad.astype(BF16).reshape(dp_count, ring, slice_rows, columns).transpose(1, 0, 2, 3)
        return to_places_dp(sum_sequence(parts))

    qkv_split = w_qkv.reshape(slice_rows, 3, dp_count, groups, pair_width).transpose(2, 0, 3, 1, 4)
    qkv_part = my_columns(qkv_split.reshape(dp_count, slice_rows, 3 * dp_width))
    qkv_weight = all_rows(lax.all_gather(qkv_part, SEQ_AXES, axis=0, tiled=False))
    in_part = my_columns(w_in.reshape(slice_rows, dp_count, inner).transpose(1, 0, 2))
    in_part = in_part.reshape(-1, width)
    in_rows, out_rows = in_part.shape[0], w_out.shape[0]
    rest = jnp.concatenate([in_part, w_out, w_dense], axis=0)
    rest = lax.all_gather(rest, SEQ_AXES, axis=0, tiled=False)
    in_weight = all_rows(rest[:, :in_rows].reshape(ring, dp_count * slice_rows, inner))
    out_weight = rest[:, in_rows : in_rows + out_rows].reshape(inner, width)
    dense_part = rest[:, in_rows + out_rows :].reshape(dp_width, width)
    dense_weight = jnp.concatenate(gather_dp(dense_part), axis=0)

    rows_in = inputs.astype(F32)
    normed_one = norm_rows(tokens.astype(F32), gains_row[0], offsets[0]).astype(BF16)
    own_offset = lax.dynamic_slice_in_dim(offsets, dp_place * dp_width, dp_width, 1)
    own_offset = own_offset.reshape(6, groups, pair_width)
    qkv_offset = jnp.stack([own_offset[1], jnp.zeros_like(own_offset[1]), own_offset[2]], axis=1).reshape(-1)
    projected = (dot_nn(normed_one, qkv_weight) + qkv_offset).astype(BF16)
    qkv = spread(projected.reshape(dp_count, rows, groups, 3 * pair_width))
    group = lax.axis_index(pair_axes) % groups
    slopes = lax.dynamic_slice_in_dim(alibi_slopes, dp_place * dp_heads + group * pair_heads, pair_heads)
    if whole_pairs:
        block = min(512, ring * rows)
        context, *kept = attend_forward(slopes, qkv, pair_heads, block)
    else:
        context, *kept = split_forward(slopes, qkv, pair_heads, rows)
    context_tok = collect(context).reshape(dp_count, rows, dp_width)
    context_tok = jnp.concatenate(swap_dp([context_tok[k] for k in range(dp_count)]), axis=1)
    middle = rows_in + (dot_nn(context_tok, dense_weight) + offsets[3])
    normed_two = norm_rows(middle, gains_row[1], offsets[4]).astype(BF16)
    normed_two_all = jnp.concatenate(gather_dp(normed_two), axis=0)
    hidden_pre = dot_nn(normed_two_all, in_weight) + in_offset
    hidden, gelu_pull = jax.vjp(jax.nn.gelu, hidden_pre)
    hidden = hidden.astype(BF16)

    grad_top = upstream.astype(F32)
    grad_pre = gelu_pull(dot_nt(grad_tokens, out_weight))[0].astype(BF16)
    grad_normed_two = sum_dp(list(dot_nt(grad_pre, in_weight).reshape(dp_count, rows, width)))
    _, second_pull = jax.vjp(norm_rows, middle, gains_row[1], offsets[4])
    grad_mid_part, grad_gain_two, grad_shift_two = second_pull(grad_normed_two)
    grad_middle = grad_top + grad_mid_part
    grad_att = grad_middle.astype(BF16)
    grad_context = dot_nt(grad_att, dense_weight).astype(BF16)
    grad_context = swap_dp([grad_context[:, k * dp_width : (k + 1) * dp_width] for k in range(dp_count)])
    grad_held = spread(jnp.stack(grad_context).reshape(dp_count, rows, groups, pair_width))

    branch = sum_dp(list(dot_nn(hidden, out_weight).reshape(dp_count, rows, width)))
    output = (middle + (branch + offsets[5])).astype(BF16)
    grad_out = dot_tn(hidden, grad_tokens).astype(BF16)
    grad_w_out = sum_sequence(grad_out.reshape(ring, -1, width)).astype(F32)
    grad_w_in = columns_gradient(dot_tn(normed_two_all, grad_pre))
    grad_w_in = grad_w_in.transpose(1, 0, 2).reshape(slice_rows, -1).astype(F32)
    grad_dense = sum_dp(list(dot_tn(context_tok, grad_att).reshape(dp_count, dp_width, width)))
    grad_w_dense = sum_sequence(grad_dense.reshape(ring, -1, width)).astype(F32)

    if whole_pairs:
        grad_qkv = attend_backward(slopes, qkv, grad_held, *kept, pair_heads, block)
    else:
        grad_qkv = split_backward(slopes, qkv, grad_held, *kept, pair_heads, rows)
    grad_projected = collect(grad_qkv).reshape(dp_count * rows, 3 * dp_width)
    grad_w_qkv = columns_gradient(dot_tn(normed_one, grad_projected))
    grad_w_qkv = grad_w_qkv.reshape(dp_count, slice_rows, groups, 3, pair_width).transpose(1, 3, 0, 2, 4)
    grad_w_qkv = grad_w_qkv.reshape(slice_rows, 3 * width).astype(F32)
    grad_normed_one = sum_dp(list(dot_nt(grad_projected, qkv_weight).reshape(dp_count, rows, width)))
    _, first_pull = jax.vjp(norm_rows, rows_in, gains_row[0], offsets[0])
    grad_rows_part, grad_gain_one, grad_shift_one = first_pull(grad_normed_one)
    grad_inputs = grad_middle + grad_rows_part

    own_sums = jnp.sum(grad_projected.astype(F32), axis=0).reshape(groups, 3, pair_width)

    def placed(part, size):
        return lax.dynamic_update_slice_in_dim(jnp.zeros(size, F32), part, dp_place * part.shape[0], 0)

    grad_vectors = jnp.stack(
        [
            grad_gain_one,
            grad_gain_two,
            grad_shift_one,
            placed(own_sums[:, 0].reshape(-1), width),
            placed(own_sums[:, 2].reshape(-1), width),
            jnp.sum(grad_att.astype(F32), axis=0),
            grad_shift_two,
            jnp.sum(grad_top, axis=0),
        ]
    )
    grad_in_part = placed(jnp.sum(grad_pre.astype(F32), axis=0), inner * dp_count)
    parts = jnp.concatenate(
        [
            grad_vectors.reshape(8, devices, -1).transpose(1, 0, 2).reshape(devices, -1),
            grad_in_part.reshape(devices, -1),
        ],
        axis=1,
    )
    parts = lax.all_to_all(parts, ALL, split_axis=0, concat_axis=0, tiled=True)
    summed = jnp.sum(parts, axis=0)
    vectors = summed[: gain_size + bias_size].reshape(8, -1)
    return (
        output,
        grad_inputs,
        grad_w_qkv,
        grad_w_dense,
        grad_w_in,
        grad_w_out,
        vectors[:2],
        vectors[2:],
        summed[gain_size + bias_size :],
    )


def solution(mesh):
    rows, columns, vector = P(ALL, None), P(None, ALL), P(ALL)
    in_specs = (rows, rows, rows, rows, rows, columns, columns, vector, P(), rows)
    out_specs = (rows, rows, rows, rows, rows, rows, columns, columns, vector)
    return jax.shard_map(
        on_device, mesh=mesh, in_specs=in_specs, out_specs=out_specs, check_vma=False
    )
```

```python
import functools
import math

import jax
import jax.numpy as jnp
from jax import lax
from jax.experimental import pallas as pl
from jax.experimental.pallas import tpu as pltpu
from jax.sharding import PartitionSpec as P

H = 16
DP = ("x", "core")
ALL = ("x", "core", "sp", "blk")
SEQ_AXES = ("sp", "blk")
F32 = jnp.float32
BF16 = jnp.bfloat16
LOG2E = 1.4426950408889634


def norm_rows(features, gain_row, offset):
    row_mean = jnp.mean(features, axis=-1, keepdims=True)
    centered = features - row_mean
    variance = jnp.mean(centered * centered, axis=-1, keepdims=True)
    return centered * lax.rsqrt(variance + 1e-05) * gain_row + offset


def dot_nn(a, b):
    return lax.dot_general(a, b, (((1,), (0,)), ((), ())), preferred_element_type=F32)


def dot_nt(a, b):
    return lax.dot_general(a, b, (((1,), (1,)), ((), ())), preferred_element_type=F32)


def dot_tn(a, b):
    return lax.dot_general(a, b, (((0,), (0,)), ((), ())), preferred_element_type=F32)


def exchange(value, bit, axis=DP):
    count = lax.axis_size(axis)
    return lax.ppermute(value, axis, [(i, i ^ bit) for i in range(count)])


def gather_dp(value):
    pieces = {0: value}
    bit = lax.axis_size(DP) // 2
    while bit:
        for place in list(pieces):
            pieces[place | bit] = exchange(pieces[place], bit)
        bit //= 2
    return [pieces[place] for place in range(len(pieces))]


def sum_bits_first(pieces):
    arrived = [exchange(piece.astype(BF16), 1) for piece in pieces[1::2]]
    return [a.astype(F32) + b.astype(F32) for a, b in zip(pieces[::2], arrived, strict=True)]


def sum_bits_rest(pieces):
    bit = 2
    while len(pieces) > 1:
        arrived = [exchange(piece.astype(BF16), bit) for piece in pieces[1::2]]
        pieces = [a.astype(F32) + b.astype(F32) for a, b in zip(pieces[::2], arrived, strict=True)]
        bit *= 2
    return pieces[0]


def swap_dp(pieces):
    return [pieces[0]] + [exchange(pieces[place], place) for place in range(1, len(pieces))]


def sum_dp(pieces):
    pieces = dict(enumerate(pieces))
    count, bit = len(pieces), 1
    while bit < count:
        for place in range(0, count, 2 * bit):
            arrived = exchange(pieces[place + bit].astype(BF16), bit)
            pieces[place] = pieces[place].astype(F32) + arrived.astype(F32)
        bit *= 2
    return pieces[0]


def to_places_dp(pieces):
    mine = lax.axis_index(DP)
    placed = pieces
    for place in range(1, pieces.shape[0]):
        other = mine ^ place
        arrived = exchange(lax.dynamic_index_in_dim(pieces, other, 0), place)
        placed = lax.dynamic_update_slice_in_dim(placed, arrived, other, 0)
    return placed


def bits_of(axis, first=1):
    bits, bit = [], first
    while bit < lax.axis_size(axis):
        bits.append((axis, bit))
        bit *= 2
    return bits


def side_of(axis, bit):
    return lax.axis_index(axis) // bit % 2


def in_order(mine, other, side, level):
    above = side == 1
    return jnp.stack([jnp.where(above, other, mine), jnp.where(above, mine, other)], axis=level)


def gather_bits(held, bits, level):
    for axis, bit in bits:
        held = in_order(held, exchange(held, bit, axis), side_of(axis, bit), level)
        level += 1
    return held, level


def sum_bits(held, bits, level):
    for axis, bit in bits:
        shape = held.shape
        halves = held.reshape(shape[:level] + (shape[level] // 2, 2) + shape[level + 1 :])
        side = side_of(axis, bit)
        sent = lax.dynamic_index_in_dim(halves, 1 - side, level + 1, keepdims=False)
        kept = lax.dynamic_index_in_dim(halves, side, level + 1, keepdims=False)
        arrived = exchange(sent.astype(BF16), bit, axis)
        held = (kept.astype(F32) + arrived.astype(F32)).astype(BF16)
    return jnp.squeeze(held, level)


def sum_sequence(parts):
    held = parts.reshape((lax.axis_size("sp"), lax.axis_size("blk")) + parts.shape[1:])
    return sum_bits(sum_bits(held, bits_of("blk"), 1), bits_of("sp"), 0)


def gather_group(value, bits):
    pieces = [value]
    for axis, bit in bits:
        pieces = pieces + [exchange(piece, bit, axis) for piece in pieces]
    return pieces


def sum_group(pieces, bits):
    for axis, bit in reversed(bits):
        half = len(pieces) // 2
        arrived = [exchange(piece.astype(BF16), bit, axis) for piece in pieces[half:]]
        pieces = [a.astype(F32) + b.astype(F32) for a, b in zip(pieces[:half], arrived, strict=True)]
    return pieces[0]


def lanes_of(rows, first, count):
    lane = lax.broadcasted_iota(jnp.int32, rows.shape, 1)
    return jnp.where((lane >= first) & (lane < first + count), rows, jnp.zeros_like(rows))


def queries_at_keys(rows, head_dim):
    return lanes_of(jnp.concatenate([rows[:, head_dim:], rows[:, :head_dim]], axis=1), head_dim, head_dim)


def score_tile(keys, queries, scale, slope, key_first, query_first, masked):
    scores = dot_nt(keys, queries) * scale
    key_row = lax.broadcasted_iota(jnp.int32, (keys.shape[0], 1), 0)
    ahead = key_first - query_first
    scores = scores + (key_row.astype(F32) * slope + ahead.astype(F32) * slope)
    if masked:
        key_place = lax.broadcasted_iota(jnp.int32, scores.shape, 0) + ahead
        query_place = lax.broadcasted_iota(jnp.int32, scores.shape, 1)
        scores = jnp.where(key_place <= query_place, scores, -1e30)
    return scores


def forward_kernel(head, last, head_dim, block, slopes_ref, qk_ref, value_ref, *refs):
    earlier, (ctx_t_ref, lse_ref) = refs[:head] if last else (), refs[head if last else 0 :][:2]
    value_t_ref = refs[-1]
    step = pl.program_id(0)
    scale = LOG2E / math.sqrt(head_dim)
    slope = slopes_ref[head] * LOG2E

    @pl.when(step == 0)
    def _():
        values_t = value_ref[...].astype(F32).T.astype(BF16)
        value_t_ref[...] = values_t[head * head_dim : (head + 1) * head_dim]

    firsts = [pl.multiple_of((2 * step + half) * block, block) for half in range(2)]
    queries = [queries_at_keys(qk_ref[pl.ds(first, block), :], head_dim) for first in firsts]

    def tile(index, running, masks):
        key_first = pl.multiple_of(index * block, block)
        keys = qk_ref[pl.ds(key_first, block), :]
        values = value_t_ref[:, pl.ds(key_first, block)]
        after = list(running)
        for half, masked in masks:
            top, total, context = running[half]
            scores = score_tile(keys, queries[half], scale, slope, key_first, firsts[half], masked)
            new_top = jnp.maximum(top, jnp.max(scores, axis=0, keepdims=True))
            exponent = jnp.exp2(scores - new_top)
            shrink = jnp.exp2(top - new_top)
            total = total * shrink + jnp.sum(exponent, axis=0, keepdims=True)
            after[half] = (new_top, total, context * shrink + dot_nn(values, exponent.astype(BF16)))
        return tuple(after)

    start = (
        jnp.full((1, block), -1e30, F32),
        jnp.zeros((1, block), F32),
        jnp.zeros((head_dim, block), F32),
    )
    both = ((0, False), (1, False))
    running = lax.fori_loop(0, 2 * step, lambda index, held: tile(index, held, both), (start, start))
    running = tile(2 * step, running, ((0, True), (1, False)))
    running = tile(2 * step + 1, running, ((1, True),))
    for first, (top, total, context) in zip(firsts, running, strict=True):
        here = pl.ds(first, block)
        context = context * (1.0 / total)
        ctx_t_ref[:, here] = context
        lse_ref[:, here] = top + jnp.log2(total)
        if last:
            heads = [ref[:, here] for ref in earlier] + [context]
            refs[-2][here, :] = jnp.concatenate(heads, axis=0).T.astype(BF16)


def backward_kernel(
    head,
    head_dim,
    block,
    slopes_ref,
    qk_ref,
    value_ref,
    grad_ref,
    ctx_t_ref,
    lse_ref,
    *refs,
):
    key_t_ref, grad_key_ref, grad_sum_ref = refs[-3:]
    width = 2 * head_dim
    later, outs = (refs[:-4], refs[-4:-3]) if head == 0 else ((), refs[:2])
    step = pl.program_id(0)
    scale = LOG2E / math.sqrt(head_dim)
    unit = 1.0 / math.sqrt(head_dim)
    slope = slopes_ref[head] * LOG2E

    @pl.when(step == 0)
    def _():
        key_t_ref[...] = qk_ref[...].astype(F32).T[head_dim:].astype(BF16)
        grad_key_ref[...] = jnp.zeros_like(grad_key_ref)
        grad_sum_ref[...] = jnp.zeros_like(grad_sum_ref)

    firsts, queries, grads, deltas, lses = [], [], [], [], []
    for half in range(2):
        first = pl.multiple_of((2 * step + half) * block, block)
        here = pl.ds(first, block)
        grad_rows = grad_ref[here, :]
        grads_t = grad_rows.astype(F32).T[head * head_dim : (head + 1) * head_dim]
        firsts.append(first)
        queries.append(queries_at_keys(qk_ref[here, :], head_dim))
        grads.append(lanes_of(grad_rows, head * head_dim, head_dim))
        deltas.append(jnp.sum(grads_t * ctx_t_ref[:, here], axis=0, keepdims=True))
        lses.append(lse_ref[:, here])

    def tile(index, running, masks):
        key_first = pl.multiple_of(index * block, block)
        here = pl.ds(key_first, block)
        keys, values, keys_t = qk_ref[here, :], value_ref[here, :], key_t_ref[:, here]
        grad_sum, grad_key = grad_sum_ref[here, :], grad_key_ref[here, :]
        after = list(running)
        for half, masked in masks:
            scores = score_tile(keys, queries[half], scale, slope, key_first, firsts[half], masked)
            weights = jnp.exp2(scores - lses[half])
            grad_weights = dot_nt(values, grads[half])
            grad_scores = (weights * (grad_weights - deltas[half])).astype(BF16)
            grad_sum = grad_sum + dot_nn(weights.astype(BF16), grads[half])
            grad_key = grad_key + dot_nn(grad_scores, queries[half])
            after[half] = running[half] + dot_nn(keys_t, grad_scores)
        grad_sum_ref[here, :] = grad_sum
        grad_key_ref[here, :] = grad_key
        return tuple(after)

    start = jnp.zeros((head_dim, block), F32)
    both = ((0, False), (1, False))
    running = lax.fori_loop(0, 2 * step, lambda index, held: tile(index, held, both), (start, start))
    running = tile(2 * step, running, ((0, True), (1, False)))
    running = tile(2 * step + 1, running, ((1, True),))
    for first, total in zip(firsts, running, strict=True):
        grad_query = jnp.concatenate([total * unit, jnp.zeros_like(total)], axis=0).T
        outs[0][pl.ds(first, block), :width] = grad_query.astype(BF16)

    @pl.when(step == pl.num_programs(0) - 1)
    def _():
        outs[0][:, :width] = outs[0][:, :width] + (grad_key_ref[...] * unit).astype(BF16)
        grad_value = grad_sum_ref[...].astype(BF16)
        if head == 0:
            outs[0][:, width:] = sum((ref[...] for ref in later), grad_value)
        else:
            outs[1][...] = grad_value


def whole(count):
    return [pl.BlockSpec(memory_space=pltpu.VMEM)] * count


def columns_spec(array, width, place):
    return pl.BlockSpec((array.shape[0], width), lambda step: (0, place))


def attend_forward(slopes, qk, first, head, heads, earlier, block):
    length, width = first.shape[0], first.shape[1] // 2
    head_dim = width // heads
    pairs = length * length // 2
    last = head == heads - 1
    taken = tuple(earlier) if last else ()
    out_shape = [jax.ShapeDtypeStruct((head_dim, length), F32), jax.ShapeDtypeStruct((1, length), F32)]
    if last:
        out_shape.append(jax.ShapeDtypeStruct((length, width), BF16))
    return pl.pallas_call(
        functools.partial(forward_kernel, head, last, head_dim, block),
        grid=(length // (2 * block),),
        out_shape=tuple(out_shape),
        in_specs=[
            pl.BlockSpec(memory_space=pltpu.SMEM),
            columns_spec(qk, width, 0),
            columns_spec(first, width, 1),
        ]
        + whole(len(taken)),
        out_specs=tuple(whole(len(out_shape))),
        scratch_shapes=[pltpu.VMEM((head_dim, length), BF16)],
        compiler_params=pltpu.CompilerParams(vmem_limit_bytes=40 << 20),
        cost_estimate=pl.CostEstimate(
            flops=64 * pairs * head_dim, bytes_accessed=16 * length * head_dim, transcendentals=pairs
        ),
        name="attend_forward",
    )(slopes, qk, first, *taken)


def attend_backward(slopes, qk, first, grad, ctx_t, lse, head, heads, later, block):
    length, width = first.shape[0], first.shape[1] // 2
    head_dim = width // heads
    pairs = length * length // 2
    taken = tuple(later) if head == 0 else ()
    out_shape = [jax.ShapeDtypeStruct(first.shape, BF16)]
    if head:
        out_shape = [jax.ShapeDtypeStruct((length, width), BF16)] * 2
    return pl.pallas_call(
        functools.partial(backward_kernel, head, head_dim, block),
        grid=(length // (2 * block),),
        out_shape=tuple(out_shape),
        in_specs=[
            pl.BlockSpec(memory_space=pltpu.SMEM),
            columns_spec(qk, width, 0),
            columns_spec(first, width, 1),
        ]
        + whole(3 + len(taken)),
        out_specs=tuple(whole(len(out_shape))),
        scratch_shapes=[
            pltpu.VMEM((head_dim, length), BF16),
            pltpu.VMEM((length, width), F32),
            pltpu.VMEM((length, width), F32),
        ],
        compiler_params=pltpu.CompilerParams(vmem_limit_bytes=40 << 20),
        cost_estimate=pl.CostEstimate(
            flops=80 * pairs * head_dim, bytes_accessed=32 * length * head_dim, transcendentals=pairs
        ),
        name="attend_backward",
    )(slopes, qk, first, grad, ctx_t, lse, *taken)


def split_scores(query_rows, row_places, key_rows, key_places, slopes, score_scale):
    scores = jnp.einsum("qhe,khe->hqk", query_rows, key_rows, preferred_element_type=F32) * score_scale
    distance = (row_places[:, None] - key_places[None, :]).astype(F32)
    scores = scores - slopes[:, None, None] * distance[None]
    return jnp.where((distance >= 0)[None], scores, -1e30)


def split_setup(qkv, heads, rows_each):
    local, width = qkv.shape[0], qkv.shape[1] // 3
    shape = (heads, width // heads)
    parts, mine = lax.axis_size("blk"), lax.axis_index("blk")
    held = lax.all_gather(qkv[:, width:], "blk", axis=0, tiled=False)
    held = held.reshape(parts, local // rows_each, rows_each, 2 * width).transpose(1, 0, 2, 3)
    held = held.reshape(parts * local, 2 * width)
    index = jnp.arange(local, dtype=jnp.int32)
    places = (index // rows_each * parts + mine) * rows_each + index % rows_each
    block = min(512, local)
    return (
        qkv[:, :width].reshape((local // block, block) + shape),
        held[:, :width].reshape((parts * local,) + shape),
        held[:, width:].reshape((parts * local,) + shape),
        places.reshape(local // block, block),
        jnp.arange(parts * local, dtype=jnp.int32),
        1.0 / math.sqrt(width // heads),
    )


def split_forward(slopes, qkv, heads, rows_each):
    queries, keys, values, places, key_places, scale = split_setup(qkv, heads, rows_each)

    def one_block(item):
        chosen, block_places = item
        scores = split_scores(chosen, block_places, keys, key_places, slopes, scale)
        top = jnp.max(scores, axis=-1, keepdims=True)
        exponent = jnp.exp(scores - top)
        total = jnp.sum(exponent, axis=-1, keepdims=True)
        weights = (exponent / total).astype(BF16)
        context = jnp.einsum("hqk,khe->qhe", weights, values, preferred_element_type=F32)
        return context.astype(BF16), top, total

    contexts, tops, totals = lax.map(one_block, (queries, places))
    return contexts.reshape(qkv.shape[0], -1), tops, totals


def split_backward(slopes, qkv, grad, tops, totals, heads, rows_each):
    queries, keys, values, places, key_places, scale = split_setup(qkv, heads, rows_each)
    grads = grad.reshape(queries.shape)

    def one_block(running, item):
        grad_keys, grad_values = running
        chosen, block_places, grad_rows, top, total = item
        scores = split_scores(chosen, block_places, keys, key_places, slopes, scale)
        weights = jnp.exp(scores - top) / total
        grad_values = grad_values + jnp.einsum(
            "hqk,qhe->khe", weights.astype(BF16), grad_rows, preferred_element_type=F32
        )
        grad_probs = jnp.einsum("qhe,khe->hqk", grad_rows, values, preferred_element_type=F32)
        grad_scores = (
            weights * (grad_probs - jnp.sum(weights * grad_probs, axis=-1, keepdims=True))
        ).astype(BF16)
        grad_query = jnp.einsum("hqk,khe->qhe", grad_scores, keys, preferred_element_type=F32) * scale
        grad_keys = (
            grad_keys
            + jnp.einsum("hqk,qhe->khe", grad_scores, chosen, preferred_element_type=F32) * scale
        )
        return (grad_keys, grad_values), grad_query.astype(BF16)

    empty = jnp.zeros(keys.shape, F32)
    (grad_keys, grad_values), grad_queries = lax.scan(
        one_block, (empty, empty), (queries, places, grads, tops, totals)
    )
    local, width = grad.shape
    both = jnp.concatenate([grad_keys.reshape(-1, width), grad_values.reshape(-1, width)], axis=1)
    parts = lax.axis_size("blk")
    both = both.reshape(local // rows_each, parts, rows_each, 2 * width).transpose(1, 0, 2, 3)
    own = lax.psum_scatter(both, "blk", scatter_dimension=0, tiled=False)
    own = own.reshape(local, 2 * width).astype(BF16)
    return jnp.concatenate([grad_queries.reshape(local, width), own], axis=1)


def on_device(
    inputs, w_qkv, w_dense, w_in, w_out, norm_gains, biases, in_bias, alibi_slopes, upstream
):
    dp_count, sp_count, blk_count = (lax.axis_size(axis) for axis in (DP, "sp", "blk"))
    dp_place = lax.axis_index(DP)
    ring = sp_count * blk_count
    devices = dp_count * ring
    rows, width = inputs.shape
    slice_rows = w_qkv.shape[0]
    head_dim = width // H
    dp_heads = H // dp_count
    dp_width = dp_heads * head_dim

    whole_pairs = ring % dp_count == 0 and dp_heads == 2 * (ring // dp_count)
    pair_axes = SEQ_AXES if whole_pairs else ("sp",)
    owners = ring if whole_pairs else sp_count
    groups = owners // dp_count
    pair_heads = dp_heads // groups
    pair_width = pair_heads * head_dim

    def spread(pieces):
        columns = pieces.shape[-1]
        sent = pieces.transpose(0, 2, 1, 3).reshape(owners * rows, columns)
        return lax.all_to_all(sent, pair_axes, split_axis=0, concat_axis=0, tiled=True)

    def collect(held):
        columns = held.shape[-1]
        got = lax.all_to_all(held, pair_axes, split_axis=0, concat_axis=0, tiled=True)
        return got.reshape(dp_count, groups, rows, columns).transpose(0, 2, 1, 3)

    def my_columns(pieces):
        return lax.all_to_all(pieces, DP, split_axis=0, concat_axis=0, tiled=True)

    split = w_qkv.reshape(slice_rows, 3, dp_count, groups, pair_heads, head_dim)

    def part_columns(query, key, value):
        lead = value.shape[:-3]
        all_values = value.reshape(lead + (groups, 1, pair_width))
        pairs = [
            jnp.concatenate([query[..., head, :], key[..., head, :]], axis=-1) for head in range(pair_heads)
        ]
        pairs[0] = jnp.concatenate([pairs[0], all_values[..., 0, :]], axis=-1)
        return [pair.reshape(lead + (-1,)) for pair in pairs]

    sizes = [2 * groups * head_dim + dp_width] + [2 * groups * head_dim] * (pair_heads - 1)
    starts = [sum(sizes[:place]) for place in range(len(sizes))]

    def cut(columns):
        return [columns[..., start : start + size] for start, size in zip(starts, sizes, strict=True)]

    qkv_split = jnp.concatenate(part_columns(split[:, 0], split[:, 1], split[:, 2]), axis=-1)
    qkv_part = my_columns(qkv_split.transpose(1, 0, 2))
    qkv_part, inputs_sent, upstream_sent, w_dense, w_in, w_out, in_bias = lax.optimization_barrier(
        (qkv_part, inputs, upstream, w_dense, w_in, w_out, in_bias)
    )
    tokens = jnp.concatenate(gather_dp(inputs_sent), axis=0)
    group_bits = bits_of("x") + [("core", 1)]
    x_count = dp_count // 2
    ff_rows = in_bias.shape[0]
    inner = ff_rows * ring
    grad_pieces = gather_group(upstream_sent, group_bits)
    small = jnp.concatenate([norm_gains.reshape(-1), biases.reshape(-1), in_bias])
    small = lax.all_to_all(
        jnp.broadcast_to(small[None], (devices, small.shape[0])), ALL, split_axis=0, concat_axis=0, tiled=True
    )
    gain_size, bias_size = norm_gains.size, biases.size
    gains_row = small[:, :gain_size].reshape(devices, 2, -1).transpose(1, 0, 2).reshape(2, width).astype(F32)
    offsets = small[:, gain_size : gain_size + bias_size].reshape(devices, 6, -1)
    offsets = offsets.transpose(1, 0, 2).reshape(6, width).astype(F32)
    in_offset = small[:, gain_size + bias_size :].reshape(dp_count, inner)
    in_offset = lax.dynamic_index_in_dim(in_offset, dp_place, 0, keepdims=False).astype(F32)

    def all_rows(gathered):
        columns = gathered.shape[-1]
        gathered = gathered.reshape(ring, dp_count, slice_rows, columns)
        return gathered.transpose(1, 0, 2, 3).reshape(width, columns)

    def by_owner(grad):
        return grad.reshape(dp_count, ring, slice_rows, -1).transpose(1, 0, 2, 3)

    def split_ring(parts):
        return parts.reshape((sp_count, blk_count) + parts.shape[1:])

    qkv_weight = all_rows(lax.all_gather(qkv_part, SEQ_AXES, axis=0, tiled=False))
    early = jnp.concatenate([w_dense, w_out], axis=0)
    early = lax.all_gather(early, SEQ_AXES, axis=0, tiled=False)
    dense_pieces = gather_dp(early[:, :slice_rows].reshape(dp_width, width))
    dense_weight = jnp.concatenate(dense_pieces, axis=0)
    out_weight = early[:, slice_rows:].reshape(inner, width)
    in_part = my_columns(w_in.reshape(slice_rows, dp_count, inner).transpose(1, 0, 2))
    in_weight = all_rows(lax.all_gather(in_part, SEQ_AXES, axis=0, tiled=False))

    rows_in = inputs.astype(F32)
    normed_one = norm_rows(tokens.astype(F32), gains_row[0], offsets[0]).astype(BF16)
    own_offset = lax.dynamic_slice_in_dim(offsets, dp_place * dp_width, dp_width, 1)
    own_offset = own_offset.reshape(6, groups, pair_heads, head_dim)
    part_offsets = part_columns(own_offset[1], jnp.zeros_like(own_offset[1]), own_offset[2])
    held = []
    for weight, offset in zip(cut(qkv_weight), part_offsets, strict=True):
        projected = (dot_nn(normed_one, weight) + offset).astype(BF16)
        held.append(spread(projected.reshape(dp_count, rows, groups, -1)))
    group = lax.axis_index(pair_axes) % groups
    slopes = lax.dynamic_slice_in_dim(alibi_slopes, dp_place * dp_heads + group * pair_heads, pair_heads)
    if whole_pairs:
        block = min(512, ring * rows // 2)
        contexts, lses = [], []
        for head in range(pair_heads):
            context_t, lse, *context = attend_forward(
                slopes, held[head], held[0], head, pair_heads, contexts, block
            )
            contexts.append(context_t)
            lses.append(lse)
        context = context[0]
    else:
        queries = [item[:, :head_dim] for item in held]
        keys = [item[:, head_dim : 2 * head_dim] for item in held]
        qkv = jnp.concatenate(queries + keys + [held[0][:, 2 * head_dim :]], axis=1)
        context, *kept = split_forward(slopes, qkv, pair_heads, rows)
    context_tok = collect(context).reshape(dp_count, rows, dp_width)
    context_tok = jnp.concatenate(swap_dp([context_tok[k] for k in range(dp_count)]), axis=1)
    middle = rows_in + (dot_nn(context_tok, dense_weight) + offsets[3])
    normed_two = norm_rows(middle, gains_row[1], offsets[4]).astype(BF16)

    grad_top = upstream.astype(F32)
    grad_in_offset, grad_out, grad_in = 0.0, 0.0, 0.0
    pieces = gather_group(normed_two, group_bits)
    branch, grad_two = [None] * len(pieces), [None] * len(pieces)
    for place in range(x_count):
        normed = jnp.concatenate(pieces[place::x_count], axis=0)
        grads = jnp.concatenate(grad_pieces[place::x_count], axis=0)
        hidden_pre = dot_nn(normed, in_weight) + in_offset
        hidden, gelu_pull = jax.vjp(jax.nn.gelu, hidden_pre)
        hidden = hidden.astype(BF16)
        grad_pre = gelu_pull(dot_nt(grads, out_weight))[0].astype(BF16)
        grad_two[place::x_count] = list(dot_nt(grad_pre, in_weight).reshape(2, rows, width))
        branch[place::x_count] = list(dot_nn(hidden, out_weight).reshape(2, rows, width))
        grad_in_offset += jnp.sum(grad_pre.astype(F32), axis=0)
        grad_out += dot_tn(hidden, grads)
        grad_in += dot_tn(normed, grad_pre)
    grad_normed_two = sum_group(grad_two, group_bits)
    grad_in = by_owner(grad_in.astype(BF16)).reshape(ring, -1, width)
    grad_out = grad_out.astype(BF16).reshape(ring, ff_rows, width)
    grad_both = jnp.concatenate([grad_in, grad_out], axis=1).reshape(-1, width)
    grad_normed_two, grad_both = lax.optimization_barrier((grad_normed_two, grad_both))
    grad_both = lax.psum_scatter(grad_both, SEQ_AXES, scatter_dimension=0, tiled=True)
    _, second_pull = jax.vjp(norm_rows, middle, gains_row[1], offsets[4])
    grad_mid_part, grad_gain_two, grad_shift_two = second_pull(grad_normed_two)
    grad_middle = grad_top + grad_mid_part
    grad_att = grad_middle.astype(BF16)
    grad_context = dot_nt(grad_att, dense_weight).astype(BF16)
    grad_context = swap_dp([grad_context[:, k * dp_width : (k + 1) * dp_width] for k in range(dp_count)])
    grad_held = spread(jnp.stack(grad_context).reshape(dp_count, rows, groups, pair_width))

    branch = sum_group(branch, group_bits)
    grad_dense = sum_dp(list(dot_tn(context_tok, grad_att).reshape(dp_count, dp_width, width)))
    grad_held, branch, grad_dense = lax.optimization_barrier((grad_held, branch, grad_dense))
    output = (middle + (branch + offsets[5])).astype(BF16)

    if whole_pairs:
        grad_qk, later = [], []
        for head in reversed(range(pair_heads)):
            grad_pair, *grad_value = attend_backward(
                slopes, held[head], held[0], grad_held, contexts[head], lses[head], head, pair_heads, later, block
            )
            grad_qk.append(grad_pair)
            later += grad_value
        grad_qk[:-1] = [collect(item) for item in grad_qk[:-1]]
        grad_qk[:-1], _ = lax.optimization_barrier((grad_qk[:-1], grad_qk[-1]))
        grad_qk[-1] = collect(grad_qk[-1])
    else:
        grad_qkv = split_backward(slopes, qkv, grad_held, *kept, pair_heads, rows)
        heads = [grad_qkv[:, start : start + head_dim] for start in range(0, 3 * pair_width, head_dim)]
        grad_qk = [
            jnp.concatenate([heads[head], heads[pair_heads + head]], axis=1)
            for head in reversed(range(pair_heads))
        ]
        grad_qk[-1] = jnp.concatenate([grad_qk[-1]] + heads[2 * pair_heads :], axis=1)
        grad_qk = [collect(item) for item in grad_qk]
    grad_parts = [item.reshape(dp_count * rows, -1) for item in grad_qk][::-1]
    later_cut = [sum_sequence(by_owner(dot_tn(normed_one, part).astype(BF16))) for part in grad_parts[1:]]
    grad_parts[0], grad_both, grad_dense = lax.optimization_barrier((grad_parts[0], grad_both, grad_dense))
    grad_dense = grad_dense.astype(BF16).reshape(ring, -1, width)
    grad_dense = lax.all_to_all(grad_dense, SEQ_AXES, split_axis=0, concat_axis=0, tiled=True)
    grad_w_dense = jnp.sum(grad_dense.astype(F32), axis=0)
    grad_one = sum(dot_nt(part, weight) for part, weight in zip(grad_parts, cut(qkv_weight), strict=True))
    grad_one = sum_bits_first(list(grad_one.reshape(dp_count, rows, width)))
    in_rows = dp_count * slice_rows * inner // width
    grad_w_out = grad_both[in_rows:].astype(F32)
    grad_in = to_places_dp(grad_both[:in_rows].reshape(dp_count, slice_rows, inner))
    grad_w_in = grad_in.transpose(1, 0, 2).reshape(slice_rows, -1).astype(F32)
    first_cut = split_ring(by_owner(dot_tn(normed_one, grad_parts[0]).astype(BF16)))
    first_cut = sum_bits(first_cut, bits_of("blk"), 1)
    first_cut, grad_one[0] = lax.optimization_barrier((first_cut, grad_one[0]))
    grad_normed_one = sum_bits_rest(grad_one)
    first_cut = sum_bits(first_cut, bits_of("sp"), 0)
    first_cut, grad_normed_one = lax.optimization_barrier((first_cut, grad_normed_one))
    grad_cut = [to_places_dp(item) for item in [first_cut] + later_cut]
    lead = (dp_count, slice_rows, groups)
    grad_cut = [item.reshape(lead + (-1, head_dim)) for item in grad_cut]
    grad_w_qkv = jnp.stack(
        [
            jnp.stack([item[..., 0, :] for item in grad_cut], axis=3),
            jnp.stack([item[..., 1, :] for item in grad_cut], axis=3),
            grad_cut[0][..., 2:, :],
        ]
    )
    grad_w_qkv = grad_w_qkv.transpose(2, 0, 1, 3, 4, 5).reshape(slice_rows, 3 * width).astype(F32)
    _, first_pull = jax.vjp(norm_rows, rows_in, gains_row[0], offsets[0])
    grad_rows_part, grad_gain_one, grad_shift_one = first_pull(grad_normed_one)
    grad_inputs = grad_middle + grad_rows_part

    part_sums = [jnp.sum(part.astype(F32), axis=0).reshape(groups, -1, head_dim) for part in grad_parts]
    query_sums = jnp.stack([item[:, 0] for item in part_sums], axis=1).reshape(-1)
    value_sums = part_sums[0][:, 2:].reshape(-1)

    def placed(part, size):
        return lax.dynamic_update_slice_in_dim(jnp.zeros(size, F32), part, dp_place * part.shape[0], 0)

    grad_vectors = jnp.stack(
        [
            grad_gain_one,
            grad_gain_two,
            grad_shift_one,
            placed(query_sums, width),
            placed(value_sums, width),
            jnp.sum(grad_att.astype(F32), axis=0),
            grad_shift_two,
            jnp.sum(grad_top, axis=0),
        ]
    )
    grad_in_part = placed(grad_in_offset, inner * dp_count)
    parts = jnp.concatenate(
        [
            grad_vectors.reshape(8, devices, -1).transpose(1, 0, 2).reshape(devices, -1),
            grad_in_part.reshape(devices, -1),
        ],
        axis=1,
    )
    parts = lax.all_to_all(parts, ALL, split_axis=0, concat_axis=0, tiled=True)
    summed = jnp.sum(parts, axis=0)
    vectors = summed[: gain_size + bias_size].reshape(8, -1)
    return (
        output,
        grad_inputs,
        grad_w_qkv,
        grad_w_dense,
        grad_w_in,
        grad_w_out,
        vectors[:2],
        vectors[2:],
        summed[gain_size + bias_size :],
    )


def solution(mesh):
    shape = mesh.devices.shape
    parted = jax.sharding.Mesh(mesh.devices.reshape((shape[0] // 2, 2) + shape[1:]), ALL)
    rows, columns, vector = P(ALL, None), P(None, ALL), P(ALL)
    in_specs = (rows, rows, rows, rows, rows, columns, columns, vector, P(), rows)
    out_specs = (rows, rows, rows, rows, rows, rows, columns, columns, vector)
    return jax.shard_map(
        on_device, mesh=parted, in_specs=in_specs, out_specs=out_specs, check_vma=False
    )
```

```python
import functools
import math

import jax
import jax.numpy as jnp
from jax import lax
from jax.experimental import pallas as pl
from jax.experimental.pallas import tpu as pltpu
from jax.sharding import PartitionSpec as P

H = 16
DP = ("x", "core")
ALL = ("x", "core", "sp", "blk")
SEQ_AXES = ("sp", "blk")
F32 = jnp.float32
BF16 = jnp.bfloat16
LOG2E = 1.4426950408889634


def norm_rows(features, gain_row, offset):
    row_mean = jnp.mean(features, axis=-1, keepdims=True)
    centered = features - row_mean
    variance = jnp.mean(centered * centered, axis=-1, keepdims=True)
    return centered * lax.rsqrt(variance + 1e-05) * gain_row + offset


def dot_nn(a, b):
    return lax.dot_general(a, b, (((1,), (0,)), ((), ())), preferred_element_type=F32)


def dot_nt(a, b):
    return lax.dot_general(a, b, (((1,), (1,)), ((), ())), preferred_element_type=F32)


def dot_tn(a, b):
    return lax.dot_general(a, b, (((0,), (0,)), ((), ())), preferred_element_type=F32)


def exchange(value, bit, axis=DP):
    count = lax.axis_size(axis)
    return lax.ppermute(value, axis, [(i, i ^ bit) for i in range(count)])


def gather_dp(value):
    pieces = {0: value}
    bit = lax.axis_size(DP) // 2
    while bit:
        for place in list(pieces):
            pieces[place | bit] = exchange(pieces[place], bit)
        bit //= 2
    return [pieces[place] for place in range(len(pieces))]


def sum_bits_first(pieces):
    arrived = [exchange(piece.astype(BF16), 1) for piece in pieces[1::2]]
    return [a.astype(F32) + b.astype(F32) for a, b in zip(pieces[::2], arrived, strict=True)]


def sum_bits_rest(pieces):
    bit = 2
    while len(pieces) > 1:
        arrived = [exchange(piece.astype(BF16), bit) for piece in pieces[1::2]]
        pieces = [a.astype(F32) + b.astype(F32) for a, b in zip(pieces[::2], arrived, strict=True)]
        bit *= 2
    return pieces[0]


def swap_dp(pieces):
    return [pieces[0]] + [exchange(pieces[place], place) for place in range(1, len(pieces))]


def sum_dp(pieces):
    pieces = dict(enumerate(pieces))
    count, bit = len(pieces), 1
    while bit < count:
        for place in range(0, count, 2 * bit):
            arrived = exchange(pieces[place + bit].astype(BF16), bit)
            pieces[place] = pieces[place].astype(F32) + arrived.astype(F32)
        bit *= 2
    return pieces[0]


def to_places_dp(pieces):
    mine = lax.axis_index(DP)
    placed = pieces
    for place in range(1, pieces.shape[0]):
        other = mine ^ place
        arrived = exchange(lax.dynamic_index_in_dim(pieces, other, 0), place)
        placed = lax.dynamic_update_slice_in_dim(placed, arrived, other, 0)
    return placed


def bits_of(axis, first=1):
    bits, bit = [], first
    while bit < lax.axis_size(axis):
        bits.append((axis, bit))
        bit *= 2
    return bits


def side_of(axis, bit):
    return lax.axis_index(axis) // bit % 2


def in_order(mine, other, side, level):
    above = side == 1
    return jnp.stack([jnp.where(above, other, mine), jnp.where(above, mine, other)], axis=level)


def gather_bits(held, bits, level):
    for axis, bit in bits:
        held = in_order(held, exchange(held, bit, axis), side_of(axis, bit), level)
        level += 1
    return held, level


def sum_bits(held, bits, level, last=True):
    for axis, bit in bits:
        shape = held.shape
        halves = held.reshape(shape[:level] + (shape[level] // 2, 2) + shape[level + 1 :])
        side = side_of(axis, bit)
        sent = lax.dynamic_index_in_dim(halves, 1 - side, level + 1, keepdims=False)
        kept = lax.dynamic_index_in_dim(halves, side, level + 1, keepdims=False)
        arrived = exchange(sent.astype(BF16), bit, axis)
        held = (kept.astype(F32) + arrived.astype(F32)).astype(BF16)
    return jnp.squeeze(held, level) if last else held


def sum_sequence(parts):
    held = parts.reshape((lax.axis_size("sp"), lax.axis_size("blk")) + parts.shape[1:])
    return sum_bits(sum_bits(held, bits_of("blk"), 1), bits_of("sp"), 0)


def gather_group(value, bits):
    pieces = [value]
    for axis, bit in bits:
        pieces = pieces + [exchange(piece, bit, axis) for piece in pieces]
    return pieces


def sum_group(pieces, bits):
    for axis, bit in reversed(bits):
        half = len(pieces) // 2
        arrived = [exchange(piece.astype(BF16), bit, axis) for piece in pieces[half:]]
        pieces = [a.astype(F32) + b.astype(F32) for a, b in zip(pieces[:half], arrived, strict=True)]
    return pieces[0]


def lanes_of(rows, first, count):
    lane = lax.broadcasted_iota(jnp.int32, rows.shape, 1)
    return jnp.where((lane >= first) & (lane < first + count), rows, jnp.zeros_like(rows))


def queries_at_keys(rows, head_dim):
    return lanes_of(jnp.concatenate([rows[:, head_dim:], rows[:, :head_dim]], axis=1), head_dim, head_dim)


def score_tile(keys, queries, scale, slope, key_first, query_first, masked):
    scores = dot_nt(keys, queries) * scale
    key_row = lax.broadcasted_iota(jnp.int32, (keys.shape[0], 1), 0)
    ahead = key_first - query_first
    scores = scores + (key_row.astype(F32) * slope + ahead.astype(F32) * slope)
    if masked:
        key_place = lax.broadcasted_iota(jnp.int32, scores.shape, 0) + ahead
        query_place = lax.broadcasted_iota(jnp.int32, scores.shape, 1)
        scores = jnp.where(key_place <= query_place, scores, -1e30)
    return scores


def forward_kernel(head, last, head_dim, block, slopes_ref, qk_ref, value_ref, *refs):
    earlier, (ctx_t_ref, lse_ref) = refs[:head] if last else (), refs[head if last else 0 :][:2]
    value_t_ref = refs[-1]
    step = pl.program_id(0)
    scale = LOG2E / math.sqrt(head_dim)
    slope = slopes_ref[head] * LOG2E

    @pl.when(step == 0)
    def _():
        values_t = value_ref[...].astype(F32).T.astype(BF16)
        value_t_ref[...] = values_t[head * head_dim : (head + 1) * head_dim]

    firsts = [pl.multiple_of((2 * step + half) * block, block) for half in range(2)]
    queries = [queries_at_keys(qk_ref[pl.ds(first, block), :], head_dim) for first in firsts]

    def tile(index, running, masks):
        key_first = pl.multiple_of(index * block, block)
        keys = qk_ref[pl.ds(key_first, block), :]
        values = value_t_ref[:, pl.ds(key_first, block)]
        after = list(running)
        for half, masked in masks:
            top, total, context = running[half]
            scores = score_tile(keys, queries[half], scale, slope, key_first, firsts[half], masked)
            new_top = jnp.maximum(top, jnp.max(scores, axis=0, keepdims=True))
            exponent = jnp.exp2(scores - new_top)
            shrink = jnp.exp2(top - new_top)
            total = total * shrink + jnp.sum(exponent, axis=0, keepdims=True)
            after[half] = (new_top, total, context * shrink + dot_nn(values, exponent.astype(BF16)))
        return tuple(after)

    start = (
        jnp.full((1, block), -1e30, F32),
        jnp.zeros((1, block), F32),
        jnp.zeros((head_dim, block), F32),
    )
    both = ((0, False), (1, False))
    running = lax.fori_loop(0, 2 * step, lambda index, held: tile(index, held, both), (start, start))
    running = tile(2 * step, running, ((0, True), (1, False)))
    running = tile(2 * step + 1, running, ((1, True),))
    for first, (top, total, context) in zip(firsts, running, strict=True):
        here = pl.ds(first, block)
        context = context * (1.0 / total)
        ctx_t_ref[:, here] = context
        lse_ref[:, here] = top + jnp.log2(total)
        if last:
            heads = [ref[:, here] for ref in earlier] + [context]
            refs[-2][here, :] = jnp.concatenate(heads, axis=0).T.astype(BF16)


def backward_kernel(
    head,
    head_dim,
    block,
    slopes_ref,
    qk_ref,
    value_ref,
    grad_ref,
    ctx_t_ref,
    lse_ref,
    *refs,
):
    key_t_ref, grad_key_ref, grad_sum_ref = refs[-3:]
    width = 2 * head_dim
    later, outs = (refs[:-4], refs[-4:-3]) if head == 0 else ((), refs[:2])
    step = pl.program_id(0)
    scale = LOG2E / math.sqrt(head_dim)
    unit = 1.0 / math.sqrt(head_dim)
    slope = slopes_ref[head] * LOG2E

    @pl.when(step == 0)
    def _():
        key_t_ref[...] = qk_ref[...].astype(F32).T[head_dim:].astype(BF16)
        grad_key_ref[...] = jnp.zeros_like(grad_key_ref)
        grad_sum_ref[...] = jnp.zeros_like(grad_sum_ref)

    firsts, queries, grads, deltas, lses = [], [], [], [], []
    for half in range(2):
        first = pl.multiple_of((2 * step + half) * block, block)
        here = pl.ds(first, block)
        grad_rows = grad_ref[here, :]
        grads_t = grad_rows.astype(F32).T[head * head_dim : (head + 1) * head_dim]
        firsts.append(first)
        queries.append(queries_at_keys(qk_ref[here, :], head_dim))
        grads.append(lanes_of(grad_rows, head * head_dim, head_dim))
        deltas.append(jnp.sum(grads_t * ctx_t_ref[:, here], axis=0, keepdims=True))
        lses.append(lse_ref[:, here])

    def tile(index, running, masks):
        key_first = pl.multiple_of(index * block, block)
        here = pl.ds(key_first, block)
        keys, values, keys_t = qk_ref[here, :], value_ref[here, :], key_t_ref[:, here]
        grad_sum, grad_key = grad_sum_ref[here, :], grad_key_ref[here, :]
        after = list(running)
        for half, masked in masks:
            scores = score_tile(keys, queries[half], scale, slope, key_first, firsts[half], masked)
            weights = jnp.exp2(scores - lses[half])
            grad_weights = dot_nt(values, grads[half])
            grad_scores = (weights * (grad_weights - deltas[half])).astype(BF16)
            grad_sum = grad_sum + dot_nn(weights.astype(BF16), grads[half])
            grad_key = grad_key + dot_nn(grad_scores, queries[half])
            after[half] = running[half] + dot_nn(keys_t, grad_scores)
        grad_sum_ref[here, :] = grad_sum
        grad_key_ref[here, :] = grad_key
        return tuple(after)

    start = jnp.zeros((head_dim, block), F32)
    both = ((0, False), (1, False))
    running = lax.fori_loop(0, 2 * step, lambda index, held: tile(index, held, both), (start, start))
    running = tile(2 * step, running, ((0, True), (1, False)))
    running = tile(2 * step + 1, running, ((1, True),))
    for first, total in zip(firsts, running, strict=True):
        grad_query = jnp.concatenate([total * unit, jnp.zeros_like(total)], axis=0).T
        outs[0][pl.ds(first, block), :width] = grad_query.astype(BF16)

    @pl.when(step == pl.num_programs(0) - 1)
    def _():
        outs[0][:, :width] = outs[0][:, :width] + (grad_key_ref[...] * unit).astype(BF16)
        grad_value = grad_sum_ref[...].astype(BF16)
        if head == 0:
            outs[0][:, width:] = sum((ref[...] for ref in later), grad_value)
        else:
            outs[1][...] = grad_value


def whole(count):
    return [pl.BlockSpec(memory_space=pltpu.VMEM)] * count


def columns_spec(array, width, place):
    return pl.BlockSpec((array.shape[0], width), lambda step: (0, place))


def attend_forward(slopes, qk, first, head, heads, earlier, block):
    length, width = first.shape[0], first.shape[1] // 2
    head_dim = width // heads
    pairs = length * length // 2
    last = head == heads - 1
    taken = tuple(earlier) if last else ()
    out_shape = [jax.ShapeDtypeStruct((head_dim, length), F32), jax.ShapeDtypeStruct((1, length), F32)]
    if last:
        out_shape.append(jax.ShapeDtypeStruct((length, width), BF16))
    return pl.pallas_call(
        functools.partial(forward_kernel, head, last, head_dim, block),
        grid=(length // (2 * block),),
        out_shape=tuple(out_shape),
        in_specs=[
            pl.BlockSpec(memory_space=pltpu.SMEM),
            columns_spec(qk, width, 0),
            columns_spec(first, width, 1),
        ]
        + whole(len(taken)),
        out_specs=tuple(whole(len(out_shape))),
        scratch_shapes=[pltpu.VMEM((head_dim, length), BF16)],
        compiler_params=pltpu.CompilerParams(vmem_limit_bytes=40 << 20),
        cost_estimate=pl.CostEstimate(
            flops=64 * pairs * head_dim, bytes_accessed=16 * length * head_dim, transcendentals=pairs
        ),
        name="attend_forward",
    )(slopes, qk, first, *taken)


def attend_backward(slopes, qk, first, grad, ctx_t, lse, head, heads, later, block):
    length, width = first.shape[0], first.shape[1] // 2
    head_dim = width // heads
    pairs = length * length // 2
    taken = tuple(later) if head == 0 else ()
    out_shape = [jax.ShapeDtypeStruct(first.shape, BF16)]
    if head:
        out_shape = [jax.ShapeDtypeStruct((length, width), BF16)] * 2
    return pl.pallas_call(
        functools.partial(backward_kernel, head, head_dim, block),
        grid=(length // (2 * block),),
        out_shape=tuple(out_shape),
        in_specs=[
            pl.BlockSpec(memory_space=pltpu.SMEM),
            columns_spec(qk, width, 0),
            columns_spec(first, width, 1),
        ]
        + whole(3 + len(taken)),
        out_specs=tuple(whole(len(out_shape))),
        scratch_shapes=[
            pltpu.VMEM((head_dim, length), BF16),
            pltpu.VMEM((length, width), F32),
            pltpu.VMEM((length, width), F32),
        ],
        compiler_params=pltpu.CompilerParams(vmem_limit_bytes=40 << 20),
        cost_estimate=pl.CostEstimate(
            flops=80 * pairs * head_dim, bytes_accessed=32 * length * head_dim, transcendentals=pairs
        ),
        name="attend_backward",
    )(slopes, qk, first, grad, ctx_t, lse, *taken)


def split_scores(query_rows, row_places, key_rows, key_places, slopes, score_scale):
    scores = jnp.einsum("qhe,khe->hqk", query_rows, key_rows, preferred_element_type=F32) * score_scale
    distance = (row_places[:, None] - key_places[None, :]).astype(F32)
    scores = scores - slopes[:, None, None] * distance[None]
    return jnp.where((distance >= 0)[None], scores, -1e30)


def split_setup(qkv, heads, rows_each):
    local, width = qkv.shape[0], qkv.shape[1] // 3
    shape = (heads, width // heads)
    parts, mine = lax.axis_size("blk"), lax.axis_index("blk")
    held = lax.all_gather(qkv[:, width:], "blk", axis=0, tiled=False)
    held = held.reshape(parts, local // rows_each, rows_each, 2 * width).transpose(1, 0, 2, 3)
    held = held.reshape(parts * local, 2 * width)
    index = jnp.arange(local, dtype=jnp.int32)
    places = (index // rows_each * parts + mine) * rows_each + index % rows_each
    block = min(512, local)
    return (
        qkv[:, :width].reshape((local // block, block) + shape),
        held[:, :width].reshape((parts * local,) + shape),
        held[:, width:].reshape((parts * local,) + shape),
        places.reshape(local // block, block),
        jnp.arange(parts * local, dtype=jnp.int32),
        1.0 / math.sqrt(width // heads),
    )


def split_forward(slopes, qkv, heads, rows_each):
    queries, keys, values, places, key_places, scale = split_setup(qkv, heads, rows_each)

    def one_block(item):
        chosen, block_places = item
        scores = split_scores(chosen, block_places, keys, key_places, slopes, scale)
        top = jnp.max(scores, axis=-1, keepdims=True)
        exponent = jnp.exp(scores - top)
        total = jnp.sum(exponent, axis=-1, keepdims=True)
        weights = (exponent / total).astype(BF16)
        context = jnp.einsum("hqk,khe->qhe", weights, values, preferred_element_type=F32)
        return context.astype(BF16), top, total

    contexts, tops, totals = lax.map(one_block, (queries, places))
    return contexts.reshape(qkv.shape[0], -1), tops, totals


def split_backward(slopes, qkv, grad, tops, totals, heads, rows_each):
    queries, keys, values, places, key_places, scale = split_setup(qkv, heads, rows_each)
    grads = grad.reshape(queries.shape)

    def one_block(running, item):
        grad_keys, grad_values = running
        chosen, block_places, grad_rows, top, total = item
        scores = split_scores(chosen, block_places, keys, key_places, slopes, scale)
        weights = jnp.exp(scores - top) / total
        grad_values = grad_values + jnp.einsum(
            "hqk,qhe->khe", weights.astype(BF16), grad_rows, preferred_element_type=F32
        )
        grad_probs = jnp.einsum("qhe,khe->hqk", grad_rows, values, preferred_element_type=F32)
        grad_scores = (
            weights * (grad_probs - jnp.sum(weights * grad_probs, axis=-1, keepdims=True))
        ).astype(BF16)
        grad_query = jnp.einsum("hqk,khe->qhe", grad_scores, keys, preferred_element_type=F32) * scale
        grad_keys = (
            grad_keys
            + jnp.einsum("hqk,qhe->khe", grad_scores, chosen, preferred_element_type=F32) * scale
        )
        return (grad_keys, grad_values), grad_query.astype(BF16)

    empty = jnp.zeros(keys.shape, F32)
    (grad_keys, grad_values), grad_queries = lax.scan(
        one_block, (empty, empty), (queries, places, grads, tops, totals)
    )
    local, width = grad.shape
    both = jnp.concatenate([grad_keys.reshape(-1, width), grad_values.reshape(-1, width)], axis=1)
    parts = lax.axis_size("blk")
    both = both.reshape(local // rows_each, parts, rows_each, 2 * width).transpose(1, 0, 2, 3)
    own = lax.psum_scatter(both, "blk", scatter_dimension=0, tiled=False)
    own = own.reshape(local, 2 * width).astype(BF16)
    return jnp.concatenate([grad_queries.reshape(local, width), own], axis=1)


def on_device(
    inputs, w_qkv, w_dense, w_in, w_out, norm_gains, biases, in_bias, alibi_slopes, upstream
):
    dp_count, sp_count, blk_count = (lax.axis_size(axis) for axis in (DP, "sp", "blk"))
    dp_place = lax.axis_index(DP)
    ring = sp_count * blk_count
    devices = dp_count * ring
    rows, width = inputs.shape
    slice_rows = w_qkv.shape[0]
    head_dim = width // H
    dp_heads = H // dp_count
    dp_width = dp_heads * head_dim

    whole_pairs = ring % dp_count == 0 and dp_heads == 2 * (ring // dp_count)
    pair_axes = SEQ_AXES if whole_pairs else ("sp",)
    owners = ring if whole_pairs else sp_count
    groups = owners // dp_count
    pair_heads = dp_heads // groups
    pair_width = pair_heads * head_dim

    def spread(pieces):
        columns = pieces.shape[-1]
        sent = pieces.transpose(0, 2, 1, 3).reshape(owners * rows, columns)
        return lax.all_to_all(sent, pair_axes, split_axis=0, concat_axis=0, tiled=True)

    def collect(held):
        columns = held.shape[-1]
        got = lax.all_to_all(held, pair_axes, split_axis=0, concat_axis=0, tiled=True)
        return got.reshape(dp_count, groups, rows, columns).transpose(0, 2, 1, 3)

    def my_columns(pieces):
        return lax.all_to_all(pieces, DP, split_axis=0, concat_axis=0, tiled=True)

    split = w_qkv.reshape(slice_rows, 3, dp_count, groups, pair_heads, head_dim)

    def part_columns(query, key, value):
        lead = value.shape[:-3]
        all_values = value.reshape(lead + (groups, 1, pair_width))
        pairs = [
            jnp.concatenate([query[..., head, :], key[..., head, :]], axis=-1) for head in range(pair_heads)
        ]
        pairs[0] = jnp.concatenate([pairs[0], all_values[..., 0, :]], axis=-1)
        return [pair.reshape(lead + (-1,)) for pair in pairs]

    sizes = [2 * groups * head_dim + dp_width] + [2 * groups * head_dim] * (pair_heads - 1)
    starts = [sum(sizes[:place]) for place in range(len(sizes))]

    def cut(columns):
        return [columns[..., start : start + size] for start, size in zip(starts, sizes, strict=True)]

    qkv_split = jnp.concatenate(part_columns(split[:, 0], split[:, 1], split[:, 2]), axis=-1)
    qkv_part = my_columns(qkv_split.transpose(1, 0, 2))
    qkv_part, inputs_sent, upstream_sent, w_dense, w_in, w_out, in_bias = lax.optimization_barrier(
        (qkv_part, inputs, upstream, w_dense, w_in, w_out, in_bias)
    )
    tokens = jnp.concatenate(gather_dp(inputs_sent), axis=0)
    group_bits = bits_of("x") + [("core", 1)]
    x_count = dp_count // 2
    ff_rows = in_bias.shape[0]
    inner = ff_rows * ring
    grad_pieces = gather_group(upstream_sent, group_bits)
    small = jnp.concatenate([norm_gains.reshape(-1), biases.reshape(-1), in_bias])
    small = lax.all_to_all(
        jnp.broadcast_to(small[None], (devices, small.shape[0])), ALL, split_axis=0, concat_axis=0, tiled=True
    )
    gain_size, bias_size = norm_gains.size, biases.size
    gains_row = small[:, :gain_size].reshape(devices, 2, -1).transpose(1, 0, 2).reshape(2, width).astype(F32)
    offsets = small[:, gain_size : gain_size + bias_size].reshape(devices, 6, -1)
    offsets = offsets.transpose(1, 0, 2).reshape(6, width).astype(F32)
    in_offset = small[:, gain_size + bias_size :].reshape(dp_count, inner)
    in_offset = lax.dynamic_index_in_dim(in_offset, dp_place, 0, keepdims=False).astype(F32)

    def all_rows(gathered):
        columns = gathered.shape[-1]
        gathered = gathered.reshape(ring, dp_count, slice_rows, columns)
        return gathered.transpose(1, 0, 2, 3).reshape(width, columns)

    def by_owner(grad):
        return grad.reshape(dp_count, ring, slice_rows, -1).transpose(1, 0, 2, 3)

    def split_ring(parts):
        return parts.reshape((sp_count, blk_count) + parts.shape[1:])

    qkv_weight = all_rows(lax.all_gather(qkv_part, SEQ_AXES, axis=0, tiled=False))
    early = jnp.concatenate([w_dense, w_out], axis=0)
    early = lax.all_gather(early, SEQ_AXES, axis=0, tiled=False)
    dense_pieces = gather_dp(early[:, :slice_rows].reshape(dp_width, width))
    dense_weight = jnp.concatenate(dense_pieces, axis=0)
    out_weight = early[:, slice_rows:].reshape(inner, width)
    in_part = my_columns(w_in.reshape(slice_rows, dp_count, inner).transpose(1, 0, 2))
    in_weight = all_rows(lax.all_gather(in_part, SEQ_AXES, axis=0, tiled=False))

    rows_in = inputs.astype(F32)
    normed_one = norm_rows(tokens.astype(F32), gains_row[0], offsets[0]).astype(BF16)
    own_offset = lax.dynamic_slice_in_dim(offsets, dp_place * dp_width, dp_width, 1)
    own_offset = own_offset.reshape(6, groups, pair_heads, head_dim)
    part_offsets = part_columns(own_offset[1], jnp.zeros_like(own_offset[1]), own_offset[2])
    held = []
    for weight, offset in zip(cut(qkv_weight), part_offsets, strict=True):
        projected = (dot_nn(normed_one, weight) + offset).astype(BF16)
        held.append(spread(projected.reshape(dp_count, rows, groups, -1)))
    group = lax.axis_index(pair_axes) % groups
    slopes = lax.dynamic_slice_in_dim(alibi_slopes, dp_place * dp_heads + group * pair_heads, pair_heads)
    if whole_pairs:
        block = min(512, ring * rows // 2)
        contexts, lses = [], []
        for head in range(pair_heads):
            context_t, lse, *context = attend_forward(
                slopes, held[head], held[0], head, pair_heads, contexts, block
            )
            contexts.append(context_t)
            lses.append(lse)
        context = context[0]
    else:
        queries = [item[:, :head_dim] for item in held]
        keys = [item[:, head_dim : 2 * head_dim] for item in held]
        qkv = jnp.concatenate(queries + keys + [held[0][:, 2 * head_dim :]], axis=1)
        context, *kept = split_forward(slopes, qkv, pair_heads, rows)
    context_tok = collect(context).reshape(dp_count, rows, dp_width)
    context_tok = jnp.concatenate(swap_dp([context_tok[k] for k in range(dp_count)]), axis=1)
    middle = rows_in + (dot_nn(context_tok, dense_weight) + offsets[3])
    normed_two = norm_rows(middle, gains_row[1], offsets[4]).astype(BF16)

    grad_top = upstream.astype(F32)
    grad_in_offset, grad_out, grad_in = 0.0, 0.0, 0.0
    pieces = gather_group(normed_two, group_bits)
    branch, grad_two, hiddens = [None] * len(pieces), [None] * len(pieces), []
    for place in range(x_count):
        normed = jnp.concatenate(pieces[place::x_count], axis=0)
        grads = jnp.concatenate(grad_pieces[place::x_count], axis=0)
        hidden_pre = dot_nn(normed, in_weight) + in_offset
        hidden, gelu_pull = jax.vjp(jax.nn.gelu, hidden_pre)
        hidden = hidden.astype(BF16)
        grad_pre = gelu_pull(dot_nt(grads, out_weight))[0].astype(BF16)
        grad_two[place::x_count] = list(dot_nt(grad_pre, in_weight).reshape(2, rows, width))
        hiddens.append(hidden)
        grad_in_offset += jnp.sum(grad_pre.astype(F32), axis=0)
        grad_out += dot_tn(hidden, grads)
        grad_in += dot_tn(normed, grad_pre)
    grad_normed_two = sum_group(grad_two, group_bits)
    grad_in = by_owner(grad_in.astype(BF16)).reshape(ring, -1, width)
    grad_out = grad_out.astype(BF16).reshape(ring, ff_rows, width)
    grad_both = jnp.concatenate([grad_in, grad_out], axis=1).reshape(-1, width)
    grad_normed_two, grad_both = lax.optimization_barrier((grad_normed_two, grad_both))
    grad_both = lax.psum_scatter(grad_both, SEQ_AXES, scatter_dimension=0, tiled=True)
    _, second_pull = jax.vjp(norm_rows, middle, gains_row[1], offsets[4])
    grad_mid_part, grad_gain_two, grad_shift_two = second_pull(grad_normed_two)
    grad_middle = grad_top + grad_mid_part
    grad_att = grad_middle.astype(BF16)
    grad_context = dot_nt(grad_att, dense_weight).astype(BF16)
    grad_context = swap_dp([grad_context[:, k * dp_width : (k + 1) * dp_width] for k in range(dp_count)])
    grad_held = spread(jnp.stack(grad_context).reshape(dp_count, rows, groups, pair_width))

    grad_held, hiddens, grad_late = lax.optimization_barrier((grad_held, hiddens, grad_att))
    for place, hidden in enumerate(hiddens):
        branch[place::x_count] = list(dot_nn(hidden, out_weight).reshape(2, rows, width))
    output = (middle + (sum_group(branch, group_bits) + offsets[5])).astype(BF16)
    grad_dense = sum_dp(list(dot_tn(context_tok, grad_late).reshape(dp_count, dp_width, width)))

    if whole_pairs:
        grad_qk, later = [], []
        for head in reversed(range(pair_heads)):
            grad_pair, *grad_value = attend_backward(
                slopes, held[head], held[0], grad_held, contexts[head], lses[head], head, pair_heads, later, block
            )
            grad_qk.append(grad_pair)
            later += grad_value
        grad_qk[:-1] = [collect(item) for item in grad_qk[:-1]]
        grad_qk[:-1], _ = lax.optimization_barrier((grad_qk[:-1], grad_qk[-1]))
        grad_qk[-1] = collect(grad_qk[-1])
    else:
        grad_qkv = split_backward(slopes, qkv, grad_held, *kept, pair_heads, rows)
        heads = [grad_qkv[:, start : start + head_dim] for start in range(0, 3 * pair_width, head_dim)]
        grad_qk = [
            jnp.concatenate([heads[head], heads[pair_heads + head]], axis=1)
            for head in reversed(range(pair_heads))
        ]
        grad_qk[-1] = jnp.concatenate([grad_qk[-1]] + heads[2 * pair_heads :], axis=1)
        grad_qk = [collect(item) for item in grad_qk]
    grad_parts = [item.reshape(dp_count * rows, -1) for item in grad_qk][::-1]
    later_sent = [by_owner(dot_tn(normed_one, part).astype(BF16)) for part in grad_parts[1:]]
    grad_parts[0], later_sent, grad_both, grad_dense = lax.optimization_barrier(
        (grad_parts[0], later_sent, grad_both, grad_dense)
    )
    grad_dense = grad_dense.astype(BF16).reshape(ring, -1, width)
    grad_dense = lax.all_to_all(grad_dense, SEQ_AXES, split_axis=0, concat_axis=0, tiled=True)
    in_rows = dp_count * slice_rows * inner // width
    grad_w_out = grad_both[in_rows:].astype(F32)
    grad_in = to_places_dp(grad_both[:in_rows].reshape(dp_count, slice_rows, inner))
    grad_w_in = grad_in.transpose(1, 0, 2).reshape(slice_rows, -1).astype(F32)
    grad_one = sum(dot_nt(part, weight) for part, weight in zip(grad_parts, cut(qkv_weight), strict=True))
    grad_one = list(grad_one.reshape(dp_count, rows, width))
    first_part, grad_one = lax.optimization_barrier((grad_parts[0], grad_one))
    grad_sent = [by_owner(dot_tn(normed_one, first_part).astype(BF16))] + later_sent
    grad_sent = jnp.concatenate(grad_sent, axis=-1)
    grad_sent, grad_dense = lax.optimization_barrier((grad_sent, grad_dense))
    grad_cut = lax.all_to_all(grad_sent, SEQ_AXES, split_axis=0, concat_axis=0, tiled=True)
    grad_normed_one = sum_dp(grad_one)
    grad_cut, grad_normed_one = lax.optimization_barrier((grad_cut, grad_normed_one))
    grad_w_dense = jnp.sum(grad_dense.astype(F32), axis=0)
    grad_cut = cut(to_places_dp(jnp.sum(grad_cut.astype(F32), axis=0).astype(BF16)))
    lead = (dp_count, slice_rows, groups)
    grad_cut = [item.reshape(lead + (-1, head_dim)) for item in grad_cut]
    grad_w_qkv = jnp.stack(
        [
            jnp.stack([item[..., 0, :] for item in grad_cut], axis=3),
            jnp.stack([item[..., 1, :] for item in grad_cut], axis=3),
            grad_cut[0][..., 2:, :],
        ]
    )
    grad_w_qkv = grad_w_qkv.transpose(2, 0, 1, 3, 4, 5).reshape(slice_rows, 3 * width).astype(F32)
    _, first_pull = jax.vjp(norm_rows, rows_in, gains_row[0], offsets[0])
    grad_rows_part, grad_gain_one, grad_shift_one = first_pull(grad_normed_one)
    grad_inputs = grad_middle + grad_rows_part

    part_sums = [jnp.sum(part.astype(F32), axis=0).reshape(groups, -1, head_dim) for part in grad_parts]
    query_sums = jnp.stack([item[:, 0] for item in part_sums], axis=1).reshape(-1)
    value_sums = part_sums[0][:, 2:].reshape(-1)

    def placed(part, size):
        return lax.dynamic_update_slice_in_dim(jnp.zeros(size, F32), part, dp_place * part.shape[0], 0)

    grad_vectors = jnp.stack(
        [
            grad_gain_one,
            grad_gain_two,
            grad_shift_one,
            placed(query_sums, width),
            placed(value_sums, width),
            jnp.sum(grad_att.astype(F32), axis=0),
            grad_shift_two,
            jnp.sum(grad_top, axis=0),
        ]
    )
    grad_in_part = placed(grad_in_offset, inner * dp_count)
    parts = jnp.concatenate(
        [
            grad_vectors.reshape(8, devices, -1).transpose(1, 0, 2).reshape(devices, -1),
            grad_in_part.reshape(devices, -1),
        ],
        axis=1,
    )
    parts = lax.all_to_all(parts, ALL, split_axis=0, concat_axis=0, tiled=True)
    summed = jnp.sum(parts, axis=0)
    vectors = summed[: gain_size + bias_size].reshape(8, -1)
    return (
        output,
        grad_inputs,
        grad_w_qkv,
        grad_w_dense,
        grad_w_in,
        grad_w_out,
        vectors[:2],
        vectors[2:],
        summed[gain_size + bias_size :],
    )


def solution(mesh):
    shape = mesh.devices.shape
    parted = jax.sharding.Mesh(mesh.devices.reshape((shape[0] // 2, 2) + shape[1:]), ALL)
    rows, columns, vector = P(ALL, None), P(None, ALL), P(ALL)
    in_specs = (rows, rows, rows, rows, rows, columns, columns, vector, P(), rows)
    out_specs = (rows, rows, rows, rows, rows, rows, columns, columns, vector)
    return jax.shard_map(
        on_device, mesh=parted, in_specs=in_specs, out_specs=out_specs, check_vma=False
    )
```

```python
import functools
import math

import jax
import jax.numpy as jnp
from jax import lax
from jax.experimental import pallas as pl
from jax.experimental.pallas import tpu as pltpu
from jax.sharding import PartitionSpec as P

H = 16
DP = ("x", "core")
ALL = ("x", "core", "sp", "blk")
SEQ_AXES = ("sp", "blk")
F32 = jnp.float32
BF16 = jnp.bfloat16
LOG2E = 1.4426950408889634


def norm_rows(features, gain_row, offset):
    row_mean = jnp.mean(features, axis=-1, keepdims=True)
    centered = features - row_mean
    variance = jnp.mean(centered * centered, axis=-1, keepdims=True)
    return centered * lax.rsqrt(variance + 1e-05) * gain_row + offset


def dot_nn(a, b):
    return lax.dot_general(a, b, (((1,), (0,)), ((), ())), preferred_element_type=F32)


def dot_nt(a, b):
    return lax.dot_general(a, b, (((1,), (1,)), ((), ())), preferred_element_type=F32)


def dot_tn(a, b):
    return lax.dot_general(a, b, (((0,), (0,)), ((), ())), preferred_element_type=F32)


def exchange(value, bit, axis=DP):
    count = lax.axis_size(axis)
    return lax.ppermute(value, axis, [(i, i ^ bit) for i in range(count)])


def gather_dp(value):
    pieces = {0: value}
    bit = lax.axis_size(DP) // 2
    while bit:
        for place in list(pieces):
            pieces[place | bit] = exchange(pieces[place], bit)
        bit //= 2
    return [pieces[place] for place in range(len(pieces))]


def sum_bits_first(pieces):
    arrived = [exchange(piece.astype(BF16), 1) for piece in pieces[1::2]]
    return [a.astype(F32) + b.astype(F32) for a, b in zip(pieces[::2], arrived, strict=True)]


def sum_bits_rest(pieces):
    bit = 2
    while len(pieces) > 1:
        arrived = [exchange(piece.astype(BF16), bit) for piece in pieces[1::2]]
        pieces = [a.astype(F32) + b.astype(F32) for a, b in zip(pieces[::2], arrived, strict=True)]
        bit *= 2
    return pieces[0]


def swap_dp(pieces):
    return [pieces[0]] + [exchange(pieces[place], place) for place in range(1, len(pieces))]


def sum_dp(pieces):
    pieces = dict(enumerate(pieces))
    count, bit = len(pieces), 1
    while bit < count:
        for place in range(0, count, 2 * bit):
            arrived = exchange(pieces[place + bit].astype(BF16), bit)
            pieces[place] = pieces[place].astype(F32) + arrived.astype(F32)
        bit *= 2
    return pieces[0]


def to_places_dp(pieces):
    mine = lax.axis_index(DP)
    placed = pieces
    for place in range(1, pieces.shape[0]):
        other = mine ^ place
        arrived = exchange(lax.dynamic_index_in_dim(pieces, other, 0), place)
        placed = lax.dynamic_update_slice_in_dim(placed, arrived, other, 0)
    return placed


def bits_of(axis, first=1):
    bits, bit = [], first
    while bit < lax.axis_size(axis):
        bits.append((axis, bit))
        bit *= 2
    return bits


def side_of(axis, bit):
    return lax.axis_index(axis) // bit % 2


def in_order(mine, other, side, level):
    above = side == 1
    return jnp.stack([jnp.where(above, other, mine), jnp.where(above, mine, other)], axis=level)


def gather_bits(held, bits, level):
    for axis, bit in bits:
        held = in_order(held, exchange(held, bit, axis), side_of(axis, bit), level)
        level += 1
    return held, level


def sum_bits(held, bits, level, last=True):
    for axis, bit in bits:
        shape = held.shape
        halves = held.reshape(shape[:level] + (shape[level] // 2, 2) + shape[level + 1 :])
        side = side_of(axis, bit)
        sent = lax.dynamic_index_in_dim(halves, 1 - side, level + 1, keepdims=False)
        kept = lax.dynamic_index_in_dim(halves, side, level + 1, keepdims=False)
        arrived = exchange(sent.astype(BF16), bit, axis)
        held = (kept.astype(F32) + arrived.astype(F32)).astype(BF16)
    return jnp.squeeze(held, level) if last else held


def sum_sequence(parts):
    held = parts.reshape((lax.axis_size("sp"), lax.axis_size("blk")) + parts.shape[1:])
    return sum_bits(sum_bits(held, bits_of("blk"), 1), bits_of("sp"), 0)


def gather_group(value, bits):
    pieces = [value]
    for axis, bit in bits:
        pieces = pieces + [exchange(piece, bit, axis) for piece in pieces]
    return pieces


def sum_group(pieces, bits):
    for axis, bit in reversed(bits):
        half = len(pieces) // 2
        arrived = [exchange(piece.astype(BF16), bit, axis) for piece in pieces[half:]]
        pieces = [a.astype(F32) + b.astype(F32) for a, b in zip(pieces[:half], arrived, strict=True)]
    return pieces[0]


def lanes_of(rows, first, count):
    lane = lax.broadcasted_iota(jnp.int32, rows.shape, 1)
    return jnp.where((lane >= first) & (lane < first + count), rows, jnp.zeros_like(rows))


def queries_at_keys(rows, head_dim):
    return lanes_of(jnp.concatenate([rows[:, head_dim:], rows[:, :head_dim]], axis=1), head_dim, head_dim)


def score_tile(keys, queries, scale, slope, key_first, query_first, masked):
    scores = dot_nt(keys, queries) * scale
    key_row = lax.broadcasted_iota(jnp.int32, (keys.shape[0], 1), 0)
    ahead = key_first - query_first
    scores = scores + (key_row.astype(F32) * slope + ahead.astype(F32) * slope)
    if masked:
        key_place = lax.broadcasted_iota(jnp.int32, scores.shape, 0) + ahead
        query_place = lax.broadcasted_iota(jnp.int32, scores.shape, 1)
        scores = jnp.where(key_place <= query_place, scores, -1e30)
    return scores


def forward_kernel(head, last, head_dim, block, slopes_ref, qk_ref, value_ref, *refs):
    earlier, (ctx_t_ref, lse_ref) = refs[:head] if last else (), refs[head if last else 0 :][:2]
    value_t_ref = refs[-1]
    step = pl.program_id(0)
    scale = LOG2E / math.sqrt(head_dim)
    slope = slopes_ref[head] * LOG2E

    @pl.when(step == 0)
    def _():
        values_t = value_ref[...].astype(F32).T.astype(BF16)
        value_t_ref[...] = values_t[head * head_dim : (head + 1) * head_dim]

    firsts = [pl.multiple_of((2 * step + half) * block, block) for half in range(2)]
    queries = [queries_at_keys(qk_ref[pl.ds(first, block), :], head_dim) for first in firsts]

    def tile(index, running, masks):
        key_first = pl.multiple_of(index * block, block)
        keys = qk_ref[pl.ds(key_first, block), :]
        values = value_t_ref[:, pl.ds(key_first, block)]
        after = list(running)
        for half, masked in masks:
            top, total, context = running[half]
            scores = score_tile(keys, queries[half], scale, slope, key_first, firsts[half], masked)
            new_top = jnp.maximum(top, jnp.max(scores, axis=0, keepdims=True))
            exponent = jnp.exp2(scores - new_top)
            shrink = jnp.exp2(top - new_top)
            total = total * shrink + jnp.sum(exponent, axis=0, keepdims=True)
            after[half] = (new_top, total, context * shrink + dot_nn(values, exponent.astype(BF16)))
        return tuple(after)

    start = (
        jnp.full((1, block), -1e30, F32),
        jnp.zeros((1, block), F32),
        jnp.zeros((head_dim, block), F32),
    )
    both = ((0, False), (1, False))
    running = lax.fori_loop(0, 2 * step, lambda index, held: tile(index, held, both), (start, start))
    running = tile(2 * step, running, ((0, True), (1, False)))
    running = tile(2 * step + 1, running, ((1, True),))
    for first, (top, total, context) in zip(firsts, running, strict=True):
        here = pl.ds(first, block)
        context = context * (1.0 / total)
        ctx_t_ref[:, here] = context
        lse_ref[:, here] = top + jnp.log2(total)
        if last:
            heads = [ref[:, here] for ref in earlier] + [context]
            refs[-2][here, :] = jnp.concatenate(heads, axis=0).T.astype(BF16)


def backward_kernel(
    head,
    head_dim,
    block,
    slopes_ref,
    qk_ref,
    value_ref,
    grad_ref,
    ctx_t_ref,
    lse_ref,
    *refs,
):
    key_t_ref, grad_key_ref, grad_sum_ref = refs[-3:]
    width = 2 * head_dim
    later, outs = (refs[:-4], refs[-4:-3]) if head == 0 else ((), refs[:2])
    step = pl.program_id(0)
    scale = LOG2E / math.sqrt(head_dim)
    unit = 1.0 / math.sqrt(head_dim)
    slope = slopes_ref[head] * LOG2E

    @pl.when(step == 0)
    def _():
        key_t_ref[...] = qk_ref[...].astype(F32).T[head_dim:].astype(BF16)
        grad_key_ref[...] = jnp.zeros_like(grad_key_ref)
        grad_sum_ref[...] = jnp.zeros_like(grad_sum_ref)

    firsts, queries, grads, deltas, lses = [], [], [], [], []
    for half in range(2):
        first = pl.multiple_of((2 * step + half) * block, block)
        here = pl.ds(first, block)
        grad_rows = grad_ref[here, :]
        grads_t = grad_rows.astype(F32).T[head * head_dim : (head + 1) * head_dim]
        firsts.append(first)
        queries.append(queries_at_keys(qk_ref[here, :], head_dim))
        grads.append(lanes_of(grad_rows, head * head_dim, head_dim))
        deltas.append(jnp.sum(grads_t * ctx_t_ref[:, here], axis=0, keepdims=True))
        lses.append(lse_ref[:, here])

    def tile(index, running, masks):
        key_first = pl.multiple_of(index * block, block)
        here = pl.ds(key_first, block)
        keys, values, keys_t = qk_ref[here, :], value_ref[here, :], key_t_ref[:, here]
        grad_sum, grad_key = grad_sum_ref[here, :], grad_key_ref[here, :]
        after = list(running)
        for half, masked in masks:
            scores = score_tile(keys, queries[half], scale, slope, key_first, firsts[half], masked)
            weights = jnp.exp2(scores - lses[half])
            grad_weights = dot_nt(values, grads[half])
            grad_scores = (weights * (grad_weights - deltas[half])).astype(BF16)
            grad_sum = grad_sum + dot_nn(weights.astype(BF16), grads[half])
            grad_key = grad_key + dot_nn(grad_scores, queries[half])
            after[half] = running[half] + dot_nn(keys_t, grad_scores)
        grad_sum_ref[here, :] = grad_sum
        grad_key_ref[here, :] = grad_key
        return tuple(after)

    start = jnp.zeros((head_dim, block), F32)
    both = ((0, False), (1, False))
    running = lax.fori_loop(0, 2 * step, lambda index, held: tile(index, held, both), (start, start))
    running = tile(2 * step, running, ((0, True), (1, False)))
    running = tile(2 * step + 1, running, ((1, True),))
    for first, total in zip(firsts, running, strict=True):
        grad_query = jnp.concatenate([total * unit, jnp.zeros_like(total)], axis=0).T
        outs[0][pl.ds(first, block), :width] = grad_query.astype(BF16)

    @pl.when(step == pl.num_programs(0) - 1)
    def _():
        outs[0][:, :width] = outs[0][:, :width] + (grad_key_ref[...] * unit).astype(BF16)
        grad_value = grad_sum_ref[...].astype(BF16)
        if head == 0:
            outs[0][:, width:] = sum((ref[...] for ref in later), grad_value)
        else:
            outs[1][...] = grad_value


def whole(count):
    return [pl.BlockSpec(memory_space=pltpu.VMEM)] * count


def columns_spec(array, width, place):
    return pl.BlockSpec((array.shape[0], width), lambda step: (0, place))


def attend_forward(slopes, qk, first, head, heads, earlier, block):
    length, width = first.shape[0], first.shape[1] // 2
    head_dim = width // heads
    pairs = length * length // 2
    last = head == heads - 1
    taken = tuple(earlier) if last else ()
    out_shape = [jax.ShapeDtypeStruct((head_dim, length), F32), jax.ShapeDtypeStruct((1, length), F32)]
    if last:
        out_shape.append(jax.ShapeDtypeStruct((length, width), BF16))
    return pl.pallas_call(
        functools.partial(forward_kernel, head, last, head_dim, block),
        grid=(length // (2 * block),),
        out_shape=tuple(out_shape),
        in_specs=[
            pl.BlockSpec(memory_space=pltpu.SMEM),
            columns_spec(qk, width, 0),
            columns_spec(first, width, 1),
        ]
        + whole(len(taken)),
        out_specs=tuple(whole(len(out_shape))),
        scratch_shapes=[pltpu.VMEM((head_dim, length), BF16)],
        compiler_params=pltpu.CompilerParams(vmem_limit_bytes=40 << 20),
        cost_estimate=pl.CostEstimate(
            flops=64 * pairs * head_dim, bytes_accessed=16 * length * head_dim, transcendentals=pairs
        ),
        name="attend_forward",
    )(slopes, qk, first, *taken)


def attend_backward(slopes, qk, first, grad, ctx_t, lse, head, heads, later, block):
    length, width = first.shape[0], first.shape[1] // 2
    head_dim = width // heads
    pairs = length * length // 2
    taken = tuple(later) if head == 0 else ()
    out_shape = [jax.ShapeDtypeStruct(first.shape, BF16)]
    if head:
        out_shape = [jax.ShapeDtypeStruct((length, width), BF16)] * 2
    return pl.pallas_call(
        functools.partial(backward_kernel, head, head_dim, block),
        grid=(length // (2 * block),),
        out_shape=tuple(out_shape),
        in_specs=[
            pl.BlockSpec(memory_space=pltpu.SMEM),
            columns_spec(qk, width, 0),
            columns_spec(first, width, 1),
        ]
        + whole(3 + len(taken)),
        out_specs=tuple(whole(len(out_shape))),
        scratch_shapes=[
            pltpu.VMEM((head_dim, length), BF16),
            pltpu.VMEM((length, width), F32),
            pltpu.VMEM((length, width), F32),
        ],
        compiler_params=pltpu.CompilerParams(vmem_limit_bytes=40 << 20),
        cost_estimate=pl.CostEstimate(
            flops=80 * pairs * head_dim, bytes_accessed=32 * length * head_dim, transcendentals=pairs
        ),
        name="attend_backward",
    )(slopes, qk, first, grad, ctx_t, lse, *taken)


def split_scores(query_rows, row_places, key_rows, key_places, slopes, score_scale):
    scores = jnp.einsum("qhe,khe->hqk", query_rows, key_rows, preferred_element_type=F32) * score_scale
    distance = (row_places[:, None] - key_places[None, :]).astype(F32)
    scores = scores - slopes[:, None, None] * distance[None]
    return jnp.where((distance >= 0)[None], scores, -1e30)


def split_setup(qkv, heads, rows_each):
    local, width = qkv.shape[0], qkv.shape[1] // 3
    shape = (heads, width // heads)
    parts, mine = lax.axis_size("blk"), lax.axis_index("blk")
    held = lax.all_gather(qkv[:, width:], "blk", axis=0, tiled=False)
    held = held.reshape(parts, local // rows_each, rows_each, 2 * width).transpose(1, 0, 2, 3)
    held = held.reshape(parts * local, 2 * width)
    index = jnp.arange(local, dtype=jnp.int32)
    places = (index // rows_each * parts + mine) * rows_each + index % rows_each
    block = min(512, local)
    return (
        qkv[:, :width].reshape((local // block, block) + shape),
        held[:, :width].reshape((parts * local,) + shape),
        held[:, width:].reshape((parts * local,) + shape),
        places.reshape(local // block, block),
        jnp.arange(parts * local, dtype=jnp.int32),
        1.0 / math.sqrt(width // heads),
    )


def split_forward(slopes, qkv, heads, rows_each):
    queries, keys, values, places, key_places, scale = split_setup(qkv, heads, rows_each)

    def one_block(item):
        chosen, block_places = item
        scores = split_scores(chosen, block_places, keys, key_places, slopes, scale)
        top = jnp.max(scores, axis=-1, keepdims=True)
        exponent = jnp.exp(scores - top)
        total = jnp.sum(exponent, axis=-1, keepdims=True)
        weights = (exponent / total).astype(BF16)
        context = jnp.einsum("hqk,khe->qhe", weights, values, preferred_element_type=F32)
        return context.astype(BF16), top, total

    contexts, tops, totals = lax.map(one_block, (queries, places))
    return contexts.reshape(qkv.shape[0], -1), tops, totals


def split_backward(slopes, qkv, grad, tops, totals, heads, rows_each):
    queries, keys, values, places, key_places, scale = split_setup(qkv, heads, rows_each)
    grads = grad.reshape(queries.shape)

    def one_block(running, item):
        grad_keys, grad_values = running
        chosen, block_places, grad_rows, top, total = item
        scores = split_scores(chosen, block_places, keys, key_places, slopes, scale)
        weights = jnp.exp(scores - top) / total
        grad_values = grad_values + jnp.einsum(
            "hqk,qhe->khe", weights.astype(BF16), grad_rows, preferred_element_type=F32
        )
        grad_probs = jnp.einsum("qhe,khe->hqk", grad_rows, values, preferred_element_type=F32)
        grad_scores = (
            weights * (grad_probs - jnp.sum(weights * grad_probs, axis=-1, keepdims=True))
        ).astype(BF16)
        grad_query = jnp.einsum("hqk,khe->qhe", grad_scores, keys, preferred_element_type=F32) * scale
        grad_keys = (
            grad_keys
            + jnp.einsum("hqk,qhe->khe", grad_scores, chosen, preferred_element_type=F32) * scale
        )
        return (grad_keys, grad_values), grad_query.astype(BF16)

    empty = jnp.zeros(keys.shape, F32)
    (grad_keys, grad_values), grad_queries = lax.scan(
        one_block, (empty, empty), (queries, places, grads, tops, totals)
    )
    local, width = grad.shape
    both = jnp.concatenate([grad_keys.reshape(-1, width), grad_values.reshape(-1, width)], axis=1)
    parts = lax.axis_size("blk")
    both = both.reshape(local // rows_each, parts, rows_each, 2 * width).transpose(1, 0, 2, 3)
    own = lax.psum_scatter(both, "blk", scatter_dimension=0, tiled=False)
    own = own.reshape(local, 2 * width).astype(BF16)
    return jnp.concatenate([grad_queries.reshape(local, width), own], axis=1)


def on_device(
    inputs, w_qkv, w_dense, w_in, w_out, norm_gains, biases, in_bias, alibi_slopes, upstream
):
    dp_count, sp_count, blk_count = (lax.axis_size(axis) for axis in (DP, "sp", "blk"))
    dp_place = lax.axis_index(DP)
    ring = sp_count * blk_count
    devices = dp_count * ring
    rows, width = inputs.shape
    slice_rows = w_qkv.shape[0]
    head_dim = width // H
    dp_heads = H // dp_count
    dp_width = dp_heads * head_dim

    whole_pairs = ring % dp_count == 0 and dp_heads == 2 * (ring // dp_count)
    pair_axes = SEQ_AXES if whole_pairs else ("sp",)
    owners = ring if whole_pairs else sp_count
    groups = owners // dp_count
    pair_heads = dp_heads // groups
    pair_width = pair_heads * head_dim

    def spread(pieces):
        columns = pieces.shape[-1]
        sent = pieces.transpose(0, 2, 1, 3).reshape(owners * rows, columns)
        return lax.all_to_all(sent, pair_axes, split_axis=0, concat_axis=0, tiled=True)

    def collect(held):
        columns = held.shape[-1]
        got = lax.all_to_all(held, pair_axes, split_axis=0, concat_axis=0, tiled=True)
        return got.reshape(dp_count, groups, rows, columns).transpose(0, 2, 1, 3)

    def my_columns(pieces):
        return lax.all_to_all(pieces, DP, split_axis=0, concat_axis=0, tiled=True)

    split = w_qkv.reshape(slice_rows, 3, dp_count, groups, pair_heads, head_dim)

    def part_columns(query, key, value):
        lead = value.shape[:-3]
        all_values = value.reshape(lead + (groups, 1, pair_width))
        pairs = [
            jnp.concatenate([query[..., head, :], key[..., head, :]], axis=-1) for head in range(pair_heads)
        ]
        pairs[0] = jnp.concatenate([pairs[0], all_values[..., 0, :]], axis=-1)
        return [pair.reshape(lead + (-1,)) for pair in pairs]

    sizes = [2 * groups * head_dim + dp_width] + [2 * groups * head_dim] * (pair_heads - 1)
    starts = [sum(sizes[:place]) for place in range(len(sizes))]

    def cut(columns):
        return [columns[..., start : start + size] for start, size in zip(starts, sizes, strict=True)]

    qkv_split = jnp.concatenate(part_columns(split[:, 0], split[:, 1], split[:, 2]), axis=-1)
    qkv_part = my_columns(qkv_split.transpose(1, 0, 2))
    qkv_part, inputs_sent, upstream_sent, w_dense, w_in, w_out, in_bias = lax.optimization_barrier(
        (qkv_part, inputs, upstream, w_dense, w_in, w_out, in_bias)
    )
    tokens = jnp.concatenate(gather_dp(inputs_sent), axis=0)
    group_bits = bits_of("x") + [("core", 1)]
    x_count = dp_count // 2
    ff_rows = in_bias.shape[0]
    inner = ff_rows * ring
    grad_pieces = gather_group(upstream_sent, group_bits)
    small = jnp.concatenate([norm_gains.reshape(-1), biases.reshape(-1), in_bias])
    small = lax.all_to_all(
        jnp.broadcast_to(small[None], (devices, small.shape[0])), ALL, split_axis=0, concat_axis=0, tiled=True
    )
    gain_size, bias_size = norm_gains.size, biases.size
    gains_row = small[:, :gain_size].reshape(devices, 2, -1).transpose(1, 0, 2).reshape(2, width).astype(F32)
    offsets = small[:, gain_size : gain_size + bias_size].reshape(devices, 6, -1)
    offsets = offsets.transpose(1, 0, 2).reshape(6, width).astype(F32)
    in_offset = small[:, gain_size + bias_size :].reshape(dp_count, inner)
    in_offset = lax.dynamic_index_in_dim(in_offset, dp_place, 0, keepdims=False).astype(F32)

    def all_rows(gathered):
        columns = gathered.shape[-1]
        gathered = gathered.reshape(ring, dp_count, slice_rows, columns)
        return gathered.transpose(1, 0, 2, 3).reshape(width, columns)

    def by_owner(grad):
        return grad.reshape(dp_count, ring, slice_rows, -1).transpose(1, 0, 2, 3)

    def split_ring(parts):
        return parts.reshape((sp_count, blk_count) + parts.shape[1:])

    qkv_weight = all_rows(lax.all_gather(qkv_part, SEQ_AXES, axis=0, tiled=False))
    early = jnp.concatenate([w_dense, w_out], axis=0)
    early = lax.all_gather(early, SEQ_AXES, axis=0, tiled=False)
    dense_pieces = gather_dp(early[:, :slice_rows].reshape(dp_width, width))
    dense_weight = jnp.concatenate(dense_pieces, axis=0)
    out_weight = early[:, slice_rows:].reshape(inner, width)
    in_part = my_columns(w_in.reshape(slice_rows, dp_count, inner).transpose(1, 0, 2))
    in_weight = all_rows(lax.all_gather(in_part, SEQ_AXES, axis=0, tiled=False))

    rows_in = inputs.astype(F32)
    normed_one = norm_rows(tokens.astype(F32), gains_row[0], offsets[0]).astype(BF16)
    own_offset = lax.dynamic_slice_in_dim(offsets, dp_place * dp_width, dp_width, 1)
    own_offset = own_offset.reshape(6, groups, pair_heads, head_dim)
    part_offsets = part_columns(own_offset[1], jnp.zeros_like(own_offset[1]), own_offset[2])
    held = []
    for weight, offset in zip(cut(qkv_weight), part_offsets, strict=True):
        projected = (dot_nn(normed_one, weight) + offset).astype(BF16)
        held.append(spread(projected.reshape(dp_count, rows, groups, -1)))
    group = lax.axis_index(pair_axes) % groups
    slopes = lax.dynamic_slice_in_dim(alibi_slopes, dp_place * dp_heads + group * pair_heads, pair_heads)
    if whole_pairs:
        block = min(512, ring * rows // 2)
        contexts, lses = [], []
        for head in range(pair_heads):
            context_t, lse, *context = attend_forward(
                slopes, held[head], held[0], head, pair_heads, contexts, block
            )
            contexts.append(context_t)
            lses.append(lse)
        context = context[0]
    else:
        queries = [item[:, :head_dim] for item in held]
        keys = [item[:, head_dim : 2 * head_dim] for item in held]
        qkv = jnp.concatenate(queries + keys + [held[0][:, 2 * head_dim :]], axis=1)
        context, *kept = split_forward(slopes, qkv, pair_heads, rows)
    context_tok = collect(context).reshape(dp_count, rows, dp_width)
    context_tok = jnp.concatenate(swap_dp([context_tok[k] for k in range(dp_count)]), axis=1)
    grads_of = [jnp.concatenate(grad_pieces[place::x_count], axis=0) for place in range(x_count)]
    grad_hidden = [dot_nt(grads, out_weight) for grads in grads_of]
    context_tok, grads_of, grad_hidden = lax.optimization_barrier((context_tok, grads_of, grad_hidden))
    middle = rows_in + (dot_nn(context_tok, dense_weight) + offsets[3])
    normed_two = norm_rows(middle, gains_row[1], offsets[4]).astype(BF16)

    grad_top = upstream.astype(F32)
    grad_in_offset, grad_out, grad_in = 0.0, 0.0, 0.0
    pieces = gather_group(normed_two, group_bits)
    branch, grad_two, hiddens = [None] * len(pieces), [None] * len(pieces), []
    for place in range(x_count):
        normed = jnp.concatenate(pieces[place::x_count], axis=0)
        grads = grads_of[place]
        hidden_pre = dot_nn(normed, in_weight) + in_offset
        hidden, gelu_pull = jax.vjp(jax.nn.gelu, hidden_pre)
        hidden = hidden.astype(BF16)
        grad_pre = gelu_pull(grad_hidden[place])[0].astype(BF16)
        grad_two[place::x_count] = list(dot_nt(grad_pre, in_weight).reshape(2, rows, width))
        hiddens.append(hidden)
        grad_in_offset += jnp.sum(grad_pre.astype(F32), axis=0)
        grad_out += dot_tn(hidden, grads)
        grad_in += dot_tn(normed, grad_pre)
    grad_normed_two = sum_group(grad_two, group_bits)
    grad_in = by_owner(grad_in.astype(BF16)).reshape(ring, -1, width)
    grad_out = grad_out.astype(BF16).reshape(ring, ff_rows, width)
    grad_both = jnp.concatenate([grad_in, grad_out], axis=1).reshape(-1, width)
    grad_normed_two, grad_both = lax.optimization_barrier((grad_normed_two, grad_both))
    grad_both = lax.psum_scatter(grad_both, SEQ_AXES, scatter_dimension=0, tiled=True)
    _, second_pull = jax.vjp(norm_rows, middle, gains_row[1], offsets[4])
    grad_mid_part, grad_gain_two, grad_shift_two = second_pull(grad_normed_two)
    grad_middle = grad_top + grad_mid_part
    grad_att = grad_middle.astype(BF16)
    grad_context = dot_nt(grad_att, dense_weight).astype(BF16)
    grad_context = swap_dp([grad_context[:, k * dp_width : (k + 1) * dp_width] for k in range(dp_count)])
    grad_held = spread(jnp.stack(grad_context).reshape(dp_count, rows, groups, pair_width))

    grad_held, hiddens, grad_late = lax.optimization_barrier((grad_held, hiddens, grad_att))
    for place, hidden in enumerate(hiddens):
        branch[place::x_count] = list(dot_nn(hidden, out_weight).reshape(2, rows, width))
    output = (middle + (sum_group(branch, group_bits) + offsets[5])).astype(BF16)
    grad_dense = sum_dp(list(dot_tn(context_tok, grad_late).reshape(dp_count, dp_width, width)))

    if whole_pairs:
        grad_qk, later = [], []
        for head in reversed(range(pair_heads)):
            grad_pair, *grad_value = attend_backward(
                slopes, held[head], held[0], grad_held, contexts[head], lses[head], head, pair_heads, later, block
            )
            grad_qk.append(grad_pair)
            later += grad_value
        grad_qk[:-1] = [collect(item) for item in grad_qk[:-1]]
        grad_qk[:-1], _ = lax.optimization_barrier((grad_qk[:-1], grad_qk[-1]))
        grad_qk[-1] = collect(grad_qk[-1])
    else:
        grad_qkv = split_backward(slopes, qkv, grad_held, *kept, pair_heads, rows)
        heads = [grad_qkv[:, start : start + head_dim] for start in range(0, 3 * pair_width, head_dim)]
        grad_qk = [
            jnp.concatenate([heads[head], heads[pair_heads + head]], axis=1)
            for head in reversed(range(pair_heads))
        ]
        grad_qk[-1] = jnp.concatenate([grad_qk[-1]] + heads[2 * pair_heads :], axis=1)
        grad_qk = [collect(item) for item in grad_qk]
    grad_parts = [item.reshape(dp_count * rows, -1) for item in grad_qk][::-1]
    later_sent = [by_owner(dot_tn(normed_one, part).astype(BF16)) for part in grad_parts[1:]]
    grad_parts[0], later_sent, grad_both, grad_dense = lax.optimization_barrier(
        (grad_parts[0], later_sent, grad_both, grad_dense)
    )
    grad_dense = grad_dense.astype(BF16).reshape(ring, -1, width)
    grad_dense = lax.all_to_all(grad_dense, SEQ_AXES, split_axis=0, concat_axis=0, tiled=True)
    in_rows = dp_count * slice_rows * inner // width
    grad_w_out = grad_both[in_rows:].astype(F32)
    grad_in = to_places_dp(grad_both[:in_rows].reshape(dp_count, slice_rows, inner))
    grad_w_in = grad_in.transpose(1, 0, 2).reshape(slice_rows, -1).astype(F32)
    grad_one = sum(dot_nt(part, weight) for part, weight in zip(grad_parts, cut(qkv_weight), strict=True))
    grad_one = list(grad_one.reshape(dp_count, rows, width))
    first_part, grad_one = lax.optimization_barrier((grad_parts[0], grad_one))
    grad_sent = [by_owner(dot_tn(normed_one, first_part).astype(BF16))] + later_sent
    grad_sent = jnp.concatenate(grad_sent, axis=-1)
    grad_sent, grad_dense = lax.optimization_barrier((grad_sent, grad_dense))
    grad_cut = lax.all_to_all(grad_sent, SEQ_AXES, split_axis=0, concat_axis=0, tiled=True)
    grad_normed_one = sum_dp(grad_one)
    grad_cut, grad_normed_one = lax.optimization_barrier((grad_cut, grad_normed_one))
    grad_w_dense = jnp.sum(grad_dense.astype(F32), axis=0)
    grad_cut = cut(to_places_dp(jnp.sum(grad_cut.astype(F32), axis=0).astype(BF16)))
    lead = (dp_count, slice_rows, groups)
    grad_cut = [item.reshape(lead + (-1, head_dim)) for item in grad_cut]
    grad_w_qkv = jnp.stack(
        [
            jnp.stack([item[..., 0, :] for item in grad_cut], axis=3),
            jnp.stack([item[..., 1, :] for item in grad_cut], axis=3),
            grad_cut[0][..., 2:, :],
        ]
    )
    grad_w_qkv = grad_w_qkv.transpose(2, 0, 1, 3, 4, 5).reshape(slice_rows, 3 * width).astype(F32)
    _, first_pull = jax.vjp(norm_rows, rows_in, gains_row[0], offsets[0])
    grad_rows_part, grad_gain_one, grad_shift_one = first_pull(grad_normed_one)
    grad_inputs = grad_middle + grad_rows_part

    part_sums = [jnp.sum(part.astype(F32), axis=0).reshape(groups, -1, head_dim) for part in grad_parts]
    query_sums = jnp.stack([item[:, 0] for item in part_sums], axis=1).reshape(-1)
    value_sums = part_sums[0][:, 2:].reshape(-1)

    def placed(part, size):
        return lax.dynamic_update_slice_in_dim(jnp.zeros(size, F32), part, dp_place * part.shape[0], 0)

    grad_vectors = jnp.stack(
        [
            grad_gain_one,
            grad_gain_two,
            grad_shift_one,
            placed(query_sums, width),
            placed(value_sums, width),
            jnp.sum(grad_att.astype(F32), axis=0),
            grad_shift_two,
            jnp.sum(grad_top, axis=0),
        ]
    )
    grad_in_part = placed(grad_in_offset, inner * dp_count)
    parts = jnp.concatenate(
        [
            grad_vectors.reshape(8, devices, -1).transpose(1, 0, 2).reshape(devices, -1),
            grad_in_part.reshape(devices, -1),
        ],
        axis=1,
    )
    parts = lax.all_to_all(parts, ALL, split_axis=0, concat_axis=0, tiled=True)
    summed = jnp.sum(parts, axis=0)
    vectors = summed[: gain_size + bias_size].reshape(8, -1)
    return (
        output,
        grad_inputs,
        grad_w_qkv,
        grad_w_dense,
        grad_w_in,
        grad_w_out,
        vectors[:2],
        vectors[2:],
        summed[gain_size + bias_size :],
    )


def solution(mesh):
    shape = mesh.devices.shape
    parted = jax.sharding.Mesh(mesh.devices.reshape((shape[0] // 2, 2) + shape[1:]), ALL)
    rows, columns, vector = P(ALL, None), P(None, ALL), P(ALL)
    in_specs = (rows, rows, rows, rows, rows, columns, columns, vector, P(), rows)
    out_specs = (rows, rows, rows, rows, rows, rows, columns, columns, vector)
    return jax.shard_map(
        on_device, mesh=parted, in_specs=in_specs, out_specs=out_specs, check_vma=False
    )
```
